512 devices in a mesh: grp: 16 (over y_hi, x, core), hist: 32 (over z, y_lo).
Axes of the slice: x: 4, y: 8 (y_hi: 2, y_lo: 4; y = y_hi * 4 + y_lo), z: 8, core: 2. Of those that a mesh axis runs over, the one named last changes fastest.
Arguments:
- cand_x: bfloat16 [512, 32, 1024], P('grp', 'hist'), may hold values from -10 to 10
- hist_kv: bfloat16 [32, 16384, 2048], P(None, 'hist', 'grp'), may hold values from -12 to 12
- hist_len: int32 [32], P('hist'), may hold values from 2048 to 16384, as said below
- cand_count: int32 [32], P('hist'), may hold values from 256 to 512, as said below
- block_mask: int32 [32, 128], P('hist'), may hold values 0 or 1
- w_proj: bfloat16 [1024, 2048], P(None, 'grp'), may hold values from -0.1875 to 0.1875
- w_out: bfloat16 [1024, 1024], P('grp'), may hold values from -0.1875 to 0.1875
Outputs:
- mixed: bfloat16 [512, 32, 1024], P('grp', 'hist')
The draws below stay inside these ranges and needn't reach their ends.
Inputs may be any that keep to these rules, and one draw needn't show every extreme that they name: `hist_len`: the number of live positions of each user's history; positions at or past it are padding. In every draw one user has all 16384 and one has 2048. `cand_count`: the number of real candidates of each user; slots at or past it are padding. In every draw one user has 512 and one has 256. `block_mask`: 1 keeps a block of 128 history positions, 0 drops it.
All inputs are finite; a program needn't handle non-finite values.
Results may differ from the reference program's by a relative error of at most 0.015.
Values may be sent and summed in bfloat16 or wider, within the bound.
No kernel may reach another device: no remote copies, remote signals or barrier semaphores. Data moves between devices by JAX's collectives and lax.ppermute only.
A program may use at most 64 MiB of HBM per device.

```python
import math
import jax
import jax.numpy as jnp
from jax import lax

D = 1024
HEADS = 16
BLK = 128
HIST = 16384
CAND = 512
USERS = 32
NBLK = 128


def scaled_levels(key, count, lowest, highest):
    return jnp.exp(jax.random.uniform(key, (count,), jnp.float32, math.log(lowest), math.log(highest)))


def draw_cand_x(key, part):
    key = jax.random.fold_in(key, 11)
    first, second, third = jax.random.split(key, 3)
    base = jnp.clip(jax.random.normal(first, (CAND, USERS, D), jnp.float32), -2.5, 2.5)
    column_gain = scaled_levels(second, D, 0.2, 2.0)
    row_gain = scaled_levels(third, CAND * USERS, 0.2, 2.0).reshape(CAND, USERS, 1)
    return (base * column_gain * row_gain).astype(jnp.bfloat16)


def draw_hist_kv(key, part):
    key = jax.random.fold_in(key, 12)
    first, second = jax.random.split(key, 2)
    head_dim = D // HEADS
    kv_shape = (USERS, HIST, HEADS, 2, head_dim)
    is_value = (jnp.arange(2) == 1).reshape(1, 1, 1, 2, 1)
    value_gain = scaled_levels(second, D, 0.3, 3.0).reshape(1, 1, HEADS, 1, head_dim)
    base = jnp.clip(jax.random.normal(first, kv_shape, jnp.float32), -4.0, 4.0)
    column_gain = jnp.where(is_value, value_gain, 1.0)
    return (base * column_gain).reshape(USERS, HIST, 2 * D).astype(jnp.bfloat16)


def draw_hist_len(key, part):
    key = jax.random.fold_in(key, 21)
    first, second = jax.random.split(key, 2)
    lowest = HIST // 8
    drawn = jax.random.randint(first, (USERS,), 0, 65)
    lengths = lowest + (HIST - lowest) * drawn * drawn // 4096
    order = jax.random.permutation(second, USERS)
    lengths = lengths.at[order[0]].set(HIST).at[order[1]].set(lowest)
    return lengths.astype(jnp.int32)


def draw_cand_count(key, part):
    key = jax.random.fold_in(key, 22)
    first, second = jax.random.split(key, 2)
    counts = jax.random.randint(first, (USERS,), CAND // 2, CAND + 1)
    order = jax.random.permutation(second, USERS)
    counts = counts.at[order[0]].set(CAND).at[order[1]].set(CAND // 2)
    return counts.astype(jnp.int32)


def with_ends(values, key, low, top_value):
    dims = values.shape
    index_at = [jax.random.randint(jax.random.fold_in(key, axis), (), 0, dims[axis]) for axis in range(len(dims))]
    values = values.at[tuple(index_at)].set(low)
    longest = dims.index(max(dims))
    index_at[longest] = (index_at[longest] + 1) % dims[longest]
    return values.at[tuple(index_at)].set(top_value)


def block_levels(own_key, extent, pieces, least, high):
    level, own = 1.0, jax.random.fold_in(own_key, 6)
    for dim, shards_of in pieces:
        draws = jnp.exp(jax.random.uniform(jax.random.fold_in(own, dim), (shards_of,), jnp.float32, least / len(pieces), high / len(pieces)))
        level = level * jnp.repeat(draws, extent[dim] // shards_of).reshape([-1 if axis == dim else 1 for axis in range(len(extent))])
    return level


def gaussian(rng, dims, width, bound, pieces=(), kind=jnp.bfloat16):
    values = width * jax.random.normal(rng, dims, jnp.float32)
    if pieces:
        values = values * block_levels(rng, dims, pieces, -0.22, 0.18)
    return jnp.clip(values, -bound, bound).astype(kind)


def setup_inputs(seed: int = 0) -> dict:
    arg_keys = jax.random.split(jax.random.key(seed), 8)
    return {
        "cand_x": draw_cand_x(jax.random.fold_in(arg_keys[7], 71), 0),
        "hist_kv": draw_hist_kv(jax.random.fold_in(arg_keys[7], 71), 0),
        "hist_len": draw_hist_len(jax.random.fold_in(arg_keys[7], 71), 0),
        "cand_count": draw_cand_count(jax.random.fold_in(arg_keys[7], 71), 0),
        "block_mask": with_ends((jax.random.randint(arg_keys[4], (USERS, NBLK), 0, 8) < 7).astype(jnp.int32), jax.random.fold_in(arg_keys[4], 1), 0, 1),
        "w_proj": gaussian(arg_keys[5], (D, 2 * D), D ** -0.5, 0.1875, ((1, 16),)),
        "w_out": gaussian(arg_keys[6], (D, D), D ** -0.5, 0.1875, ((0, 16),)),
    }


def layer_norm(values):
    average = lax.optimization_barrier(jnp.mean(values, axis=-1, keepdims=True))
    centred = values - average
    spread = lax.optimization_barrier(jnp.mean(centred * centred, axis=-1, keepdims=True))
    return centred * lax.rsqrt(spread + 1e-05)

def reference(cand_x, hist_kv, hist_len, cand_count, block_mask, w_proj, w_out):
    head_dim = D // HEADS
    inputs = cand_x.astype(jnp.float32)
    normed = layer_norm(inputs).astype(jnp.bfloat16)
    projected = jax.nn.silu(jnp.dot(normed.reshape(CAND * USERS, D), w_proj, preferred_element_type=jnp.float32)).astype(jnp.bfloat16)
    projected = projected.reshape(CAND, USERS, HEADS, 2, head_dim)
    queries = jnp.transpose(projected[:, :, :, 0, :], (1, 0, 2, 3))
    gate_part = projected[:, :, :, 1, :].reshape(CAND, USERS, D)
    key_block = math.gcd(HIST, 1024)
    blocks = HIST // key_block
    positions = jnp.arange(HIST, dtype=jnp.int32).reshape(blocks, key_block)
    score_scale = head_dim ** (-0.5)

    def one_user(operands):
        user_query, user_kv, length, mask_row = operands
        kv_blocks = user_kv.reshape(blocks, key_block, HEADS, 2, head_dim)
        live_keys = (positions < length) & (jnp.repeat(mask_row, BLK).reshape(blocks, key_block) == 1)
        query_wide = user_query.astype(jnp.float32)

        def add_block(running, operand_pair):
            kv_block, live_block = operand_pair
            key_part = kv_block[:, :, 0, :].astype(jnp.float32)
            value_part = kv_block[:, :, 1, :].astype(jnp.float32)
            scores = jnp.einsum('chd,khd->hck', query_wide, key_part) * score_scale
            weights = jnp.where(live_block[None, None, :], jax.nn.silu(scores), 0.0).astype(jnp.bfloat16)
            return (running + jnp.einsum('hck,khd->chd', weights.astype(jnp.float32), value_part), None)
        running, _ = lax.scan(add_block, jnp.zeros((CAND, HEADS, head_dim), jnp.float32), (kv_blocks, live_keys))
        return running
    attended = lax.map(one_user, (queries, hist_kv, hist_len, block_mask))
    attended = jnp.transpose(attended, (1, 0, 2, 3)).reshape(CAND, USERS, D)
    gated = (layer_norm(attended) * gate_part.astype(jnp.float32)).astype(jnp.bfloat16)
    branch = jnp.dot(gated.reshape(CAND * USERS, D), w_out, preferred_element_type=jnp.float32).reshape(CAND, USERS, D)
    mixed_out = inputs + branch
    row_index = jnp.arange(CAND, dtype=jnp.int32)[:, None]
    keep_rows = row_index < cand_count[None, :]
    return jnp.where(keep_rows[:, :, None], mixed_out, 0.0).astype(jnp.bfloat16)
```

```python
import functools

import jax
import jax.numpy as jnp
from jax import lax
from jax.experimental import pallas as pl
from jax.experimental.pallas import tpu as pltpu
from jax.sharding import PartitionSpec as P

D = 1024
BLK = 128
TILE = 256
HALF = 64
VMEM_LIMIT = 48 * 1024 * 1024


def layer_norm(values):
    average = jnp.mean(values, axis=-1, keepdims=True)
    centred = values - average
    spread = jnp.mean(centred * centred, axis=-1, keepdims=True)
    return centred * lax.rsqrt(spread + 1e-05)


def low_lanes(shape):
    return lax.broadcasted_iota(jnp.int32, shape, len(shape) - 1) < HALF


def project_kernel(rows_ref, w_ref, query_ref, gate_ref):
    product = jnp.dot(rows_ref[...], w_ref[...], preferred_element_type=jnp.float32)
    values = (product / (1.0 + jnp.exp(-product))).astype(jnp.bfloat16).astype(jnp.float32)
    query_ref[...] = jnp.where(low_lanes(values.shape), values * (0.5 * HALF ** (-0.5)), 0.0).astype(jnp.bfloat16)
    slices = values.reshape(values.shape[0] // 32, 2, 16, 128)
    first, second = slices[:, 0], slices[:, 1]
    turned = pltpu.roll(first.reshape(-1, 128), HALF, 1).reshape(first.shape)
    gate_ref[...] = jnp.where(low_lanes(first.shape), turned, second).astype(jnp.bfloat16)


def project(rows, w_proj):
    count = rows.shape[0]
    return pl.pallas_call(
        project_kernel,
        out_shape=(
            jax.ShapeDtypeStruct((count, 128), jnp.bfloat16),
            jax.ShapeDtypeStruct((count // 32, 16, 128), jnp.bfloat16),
        ),
        compiler_params=pltpu.CompilerParams(vmem_limit_bytes=VMEM_LIMIT),
        cost_estimate=pl.CostEstimate(flops=2 * count * D * 128, bytes_accessed=1 << 20, transcendentals=0),
    )(rows, w_proj)


def attend_tile(query, kv, live_first, live_second):
    scores = lax.dot_general(query, kv, (((1,), (1,)), ((), ())), preferred_element_type=jnp.float32)
    weights = (scores + scores * jnp.tanh(scores)).astype(jnp.bfloat16)
    row = lax.broadcasted_iota(jnp.int32, kv.shape, 0)
    live = row < jnp.where(row < BLK, live_first, live_second + BLK)
    values = jnp.where(live, kv, jnp.zeros_like(kv))
    return jnp.dot(weights, values, preferred_element_type=jnp.float32)


def attend_kernel(tiles, live_ref, query_ref, gate_ref, kv_ref, out_ref, total):
    step = pl.program_id(0)

    @pl.when(step == 0)
    def _():
        total[...] = jnp.zeros_like(total)

    for tile in range(tiles):
        block = (step * tiles + tile) * 2
        live_first, live_second = live_ref[block], live_ref[block + 1]

        @pl.when(live_first + live_second > 0)
        def _():
            kv = kv_ref[pl.ds(tile * TILE, TILE), :]
            total[...] += attend_tile(query_ref[...], kv, live_first, live_second)

    @pl.when(step == pl.num_programs(0) - 1)
    def _():
        slices = total[...].reshape(out_ref.shape[0], 2, 16, 128)
        first, second = slices[:, 0], slices[:, 1]
        turned = pltpu.roll(first.reshape(-1, 128), HALF, 1).reshape(first.shape)
        out_ref[:, 0:16, :] = jnp.where(low_lanes(first.shape), turned, second).astype(jnp.bfloat16)
        out_ref[:, 16:32, :] = gate_ref[...]


def attend(live, query, gate, kv):
    count = query.shape[0]
    positions = kv.shape[0]
    tiles = 4
    steps = positions // (tiles * TILE)
    return pl.pallas_call(
        functools.partial(attend_kernel, tiles),
        out_shape=jax.ShapeDtypeStruct((count // 32, 32, 128), jnp.bfloat16),
        grid=(steps,),
        in_specs=[
            pl.BlockSpec(memory_space=pltpu.SMEM),
            pl.BlockSpec((count, 128), lambda i: (0, 0)),
            pl.BlockSpec((count // 32, 16, 128), lambda i: (0, 0, 0)),
            pl.BlockSpec((tiles * TILE, 128), lambda i: (i, 0)),
        ],
        out_specs=pl.BlockSpec((count // 32, 32, 128), lambda i: (0, 0, 0)),
        scratch_shapes=[pltpu.VMEM((count, 128), jnp.float32)],
        compiler_params=pltpu.CompilerParams(vmem_limit_bytes=VMEM_LIMIT),
        cost_estimate=pl.CostEstimate(flops=4 * count * positions * 128, bytes_accessed=4 << 20, transcendentals=count * positions),
    )(live, query, gate, kv)


def spread_heads(packed):
    columns = []
    for pair in range(packed.shape[0] // 2):
        even, odd = packed[2 * pair], packed[2 * pair + 1]
        low = low_lanes(even.shape)
        top = jnp.where(low, even, pltpu.roll(odd, HALF, 1))
        bottom = jnp.where(low, pltpu.roll(even, HALF, 1), odd)
        columns.append(jnp.concatenate([top, bottom], axis=0))
    return jnp.concatenate(columns, axis=1)


def output_kernel(count_ref, parts_ref, w_ref, x_ref, out_ref):
    attended = spread_heads(parts_ref[:, 0:16, :].astype(jnp.float32))
    gate = spread_heads(parts_ref[:, 16:32, :].astype(jnp.float32))
    gated = (layer_norm(attended) * gate).astype(jnp.bfloat16)
    branch = jnp.dot(gated, w_ref[...], preferred_element_type=jnp.float32)
    mixed = x_ref[...].astype(jnp.float32) + branch
    row = lax.broadcasted_iota(jnp.int32, mixed.shape, 0)
    out_ref[...] = jnp.where(row < count_ref[0], mixed, 0.0).astype(jnp.bfloat16)


def output(keep, parts, w_out, rows):
    return pl.pallas_call(
        output_kernel,
        out_shape=jax.ShapeDtypeStruct(rows.shape, jnp.bfloat16),
        in_specs=[
            pl.BlockSpec(memory_space=pltpu.SMEM),
            pl.BlockSpec(memory_space=pltpu.VMEM),
            pl.BlockSpec(memory_space=pltpu.VMEM),
            pl.BlockSpec(memory_space=pltpu.VMEM),
        ],
        out_specs=pl.BlockSpec(memory_space=pltpu.VMEM),
        compiler_params=pltpu.CompilerParams(vmem_limit_bytes=VMEM_LIMIT),
        cost_estimate=pl.CostEstimate(flops=2 * 32 * D * D, bytes_accessed=3 << 20, transcendentals=0),
    )(keep, parts, w_out, rows)


def per_device(cand_x, hist_kv, hist_len, cand_count, block_mask, w_proj, w_out):
    own_rows = cand_x.shape[0]
    rows = cand_x.reshape(own_rows, D)
    histories = lax.all_to_all(hist_kv, "hist", split_axis=0, concat_axis=0, tiled=True)
    normed = layer_norm(rows.astype(jnp.float32)).astype(jnp.bfloat16)
    all_rows = lax.all_gather(normed, "grp", axis=0, tiled=True)
    w_out, all_rows = lax.optimization_barrier((w_out, all_rows))
    w_full = lax.all_gather(w_out, "grp", axis=0, tiled=True)
    query, gate = project(all_rows, w_proj)
    starts = jnp.arange(block_mask.shape[1], dtype=jnp.int32) * BLK
    live = jnp.clip(hist_len[0] - starts, 0, BLK) * block_mask[0]
    attended = attend(live, query, gate, histories.reshape(-1, 128))
    parts = lax.all_to_all(attended, "grp", split_axis=0, concat_axis=0, tiled=True)
    keep = cand_count - lax.axis_index("grp") * own_rows
    return output(keep, parts, w_full, rows).reshape(cand_x.shape)


def solution(mesh):
    in_specs = (
        P("grp", "hist", None),
        P(None, "hist", "grp"),
        P("hist"),
        P("hist"),
        P("hist", None),
        P(None, "grp"),
        P("grp", None),
    )
    out_specs = P("grp", "hist", None)
    return jax.shard_map(per_device, mesh=mesh, in_specs=in_specs, out_specs=out_specs, check_vma=False)
```

```python
import functools

import jax
import jax.numpy as jnp
from jax import lax
from jax.experimental import pallas as pl
from jax.experimental.pallas import tpu as pltpu
from jax.sharding import Mesh
from jax.sharding import PartitionSpec as P

D = 1024
BLK = 128
HALF = 64
PIECE = 256
TILE = 4
GRP = ("yh", "x", "c")
VMEM_LIMIT = 48 * 1024 * 1024
PARAMS = pltpu.CompilerParams(vmem_limit_bytes=VMEM_LIMIT)


def layer_norm(values):
    average = jnp.mean(values, axis=-1, keepdims=True)
    centred = values - average
    spread = jnp.mean(centred * centred, axis=-1, keepdims=True)
    return centred * lax.rsqrt(spread + 1e-05)


def low_lanes(shape):
    return lax.broadcasted_iota(jnp.int32, shape, len(shape) - 1) < HALF


def turn(values):
    return pltpu.roll(values, HALF, 1)


def norm_kernel(x_ref, out_ref):
    normed = layer_norm(x_ref[...].astype(jnp.float32)).astype(jnp.bfloat16)
    for copy in range(out_ref.shape[0]):
        out_ref[copy] = normed


def norm(rows, copies):
    return pl.pallas_call(
        norm_kernel,
        out_shape=jax.ShapeDtypeStruct((copies,) + rows.shape, jnp.bfloat16),
        compiler_params=PARAMS,
        cost_estimate=pl.CostEstimate(flops=1 << 20, bytes_accessed=1 << 20, transcendentals=0),
        name="norm",
    )(rows)


def project_kernel(length_ref, rows_ref, w_ref, mask_ref, along_z_ref, along_y_ref, gate_ref):
    slices, own, width = rows_ref.shape
    rows = rows_ref[...].reshape(slices * own, width)
    product = jnp.dot(rows, w_ref[...], preferred_element_type=jnp.float32)
    values = (product / (1.0 + jnp.exp(-product))).astype(jnp.bfloat16).astype(jnp.float32)
    values = values.reshape(slices, 2, own // 2, 128)
    first = values[:, 0].reshape(PIECE, 128)
    second = values[:, 1].reshape(PIECE, 128)
    low = low_lanes(first.shape)
    gate_ref[...] = jnp.where(low, turn(first), second).astype(jnp.bfloat16).reshape(gate_ref.shape)
    queries = (jnp.where(low, first, turn(second)) * (0.5 * HALF ** (-0.5))).astype(jnp.bfloat16)
    block = lax.broadcasted_iota(jnp.int32, mask_ref.shape, 1)
    live = jnp.clip(length_ref[0] - block * BLK, 0, BLK) * mask_ref[...]
    tail = jnp.broadcast_to(live, (16, 128)).astype(jnp.float32).astype(jnp.bfloat16)
    for ref in (along_z_ref, along_y_ref):
        for copy in range(ref.shape[0]):
            ref[copy, 0:PIECE] = queries
            ref[copy, PIECE : PIECE + 16] = tail


def project(length, rows, w_proj, mask, z_size, y_size):
    vmem = pl.BlockSpec(memory_space=pltpu.VMEM)
    return pl.pallas_call(
        project_kernel,
        out_shape=(
            jax.ShapeDtypeStruct((z_size, PIECE + 16, 128), jnp.bfloat16),
            jax.ShapeDtypeStruct((y_size, PIECE + 16, 128), jnp.bfloat16),
            jax.ShapeDtypeStruct((rows.shape[0], 16, 128), jnp.bfloat16),
        ),
        in_specs=[pl.BlockSpec(memory_space=pltpu.SMEM), vmem, vmem, vmem],
        out_specs=(vmem, vmem, vmem),
        compiler_params=PARAMS,
        cost_estimate=pl.CostEstimate(flops=2 * 512 * D * 128, bytes_accessed=2 << 20, transcendentals=0),
        name="project",
    )(length, rows, w_proj, mask)


def attend_kernel(pieces, live_ref, message_ref, *refs):
    kv_refs, (out_ref, query, kv, total) = refs[:pieces], refs[pieces:]
    user = pl.program_id(0)
    packed = message_ref[0, 0:PIECE].astype(jnp.float32)
    low = low_lanes(packed.shape)
    query[0] = jnp.where(low, packed, 0.0).astype(jnp.bfloat16)
    query[1] = jnp.where(low, turn(packed), 0.0).astype(jnp.bfloat16)
    total[...] = jnp.zeros_like(total)
    row = lax.broadcasted_iota(jnp.int32, (PIECE, 128), 0)
    for tile in range(pieces // TILE):
        base = (user * pieces + tile * TILE) * 2
        lives = [live_ref[base + i] for i in range(2 * TILE)]

        @pl.when(functools.reduce(jnp.add, lives) > 0)
        def _():
            for i in range(TILE):
                piece = kv_refs[tile * TILE + i][0]
                keep = row < jnp.where(row < BLK, lives[2 * i], lives[2 * i + 1] + BLK)
                kv[i * PIECE : (i + 1) * PIECE] = jnp.where(keep, piece, jnp.zeros_like(piece))
            for half in range(2):
                scores = lax.dot_general(
                    query[half], kv[...], (((1,), (1,)), ((), ())), preferred_element_type=jnp.float32
                )
                weights = (scores + scores * jnp.tanh(scores)).astype(jnp.bfloat16)
                total[half] += jnp.dot(weights, kv[...], preferred_element_type=jnp.float32)

    result = jnp.where(low, turn(total[0]), total[1]).astype(jnp.bfloat16)
    out_ref[...] = result.reshape(out_ref.shape)


def attend(live, messages, pieces, out_shape, out_block, out_index, name):
    users = messages.shape[0]
    count = len(pieces)
    return pl.pallas_call(
        functools.partial(attend_kernel, count),
        out_shape=jax.ShapeDtypeStruct(out_shape, jnp.bfloat16),
        grid=(users,),
        in_specs=[
            pl.BlockSpec(memory_space=pltpu.SMEM),
            pl.BlockSpec((1, PIECE + 16, 128), lambda u: (u, 0, 0)),
        ]
        + [pl.BlockSpec((1, PIECE, 128), lambda u: (u, 0, 0)) for _ in pieces],
        out_specs=pl.BlockSpec(out_block, out_index),
        scratch_shapes=[
            pltpu.VMEM((2, PIECE, 128), jnp.bfloat16),
            pltpu.VMEM((TILE * PIECE, 128), jnp.bfloat16),
            pltpu.VMEM((2, PIECE, 128), jnp.float32),
        ],
        compiler_params=PARAMS,
        cost_estimate=pl.CostEstimate(
            flops=users * count * PIECE * 512 * 512, bytes_accessed=3 << 20, transcendentals=users * count * PIECE * 512
        ),
        name=name,
    )(live, messages, *pieces)


def spread_heads(packed):
    columns = []
    for pair in range(packed.shape[0] // 2):
        even, odd = packed[2 * pair], packed[2 * pair + 1]
        low = low_lanes(even.shape)
        top = jnp.where(low, even, turn(odd))
        bottom = jnp.where(low, turn(even), odd)
        columns.append(jnp.concatenate([top, bottom], axis=0))
    return jnp.concatenate(columns, axis=1)


def output_kernel(count_ref, parts_ref, gate_ref, w_ref, x_ref, out_ref):
    attended = spread_heads(jnp.sum(parts_ref[...].astype(jnp.float32), axis=1))
    gate = spread_heads(gate_ref[...].astype(jnp.float32))
    gated = (layer_norm(attended) * gate).astype(jnp.bfloat16)
    branch = jnp.dot(gated, w_ref[...], preferred_element_type=jnp.float32)
    mixed = x_ref[...].astype(jnp.float32) + branch
    row = lax.broadcasted_iota(jnp.int32, mixed.shape, 0)
    out_ref[...] = jnp.where(row < count_ref[0], mixed, 0.0).astype(jnp.bfloat16)


def output(keep, parts, gate, w_out, rows):
    vmem = pl.BlockSpec(memory_space=pltpu.VMEM)
    return pl.pallas_call(
        output_kernel,
        out_shape=jax.ShapeDtypeStruct(rows.shape, jnp.bfloat16),
        in_specs=[pl.BlockSpec(memory_space=pltpu.SMEM), vmem, vmem, vmem, vmem],
        out_specs=vmem,
        compiler_params=PARAMS,
        cost_estimate=pl.CostEstimate(flops=2 * 32 * D * D, bytes_accessed=3 << 20, transcendentals=0),
        name="output",
    )(keep, parts, gate, w_out, rows)


def exchange(values, axes):
    return lax.all_to_all(values, axes, split_axis=0, concat_axis=0, tiled=True)


def per_device(sizes, cand_x, hist_kv, hist_len, cand_count, block_mask, w_proj, w_out):
    n_grp, n_z, n_y = sizes
    z, y = lax.axis_index("z"), lax.axis_index("yl")
    own_rows = cand_x.shape[0]
    rows = cand_x.reshape(own_rows, D)
    w_full = lax.all_gather(w_out, GRP, axis=0, tiled=True)
    all_rows = exchange(norm(rows, n_grp), GRP)

    kv = hist_kv.reshape(n_z, n_y, 2, PIECE, 128)
    along_y = [lax.dynamic_index_in_dim(kv[:, :, 0], y, 1, keepdims=False)]
    for step in range(1, n_y):
        piece = lax.dynamic_index_in_dim(kv[:, :, 0], y ^ step, 1, keepdims=False)
        along_y.append(lax.ppermute(piece, "yl", [(i, i ^ step) for i in range(n_y)]))
    along_z = [lax.dynamic_index_in_dim(kv[:, :, 1], z, 0, keepdims=False)]
    for step in range(1, n_z):
        piece = lax.dynamic_index_in_dim(kv[:, :, 1], (z + step) % n_z, 0, keepdims=False)
        along_z.append(lax.ppermute(piece, "z", [(i, (i + step) % n_z) for i in range(n_z)]))

    to_z, to_y, gate = project(hist_len, all_rows, w_proj, block_mask, n_z, n_y)
    from_z = exchange(to_z, "z")
    from_y = exchange(to_y, "yl")
    gates = exchange(gate, GRP)

    live_y = from_y[:, PIECE].astype(jnp.int32).reshape(n_y, n_z, n_y, 4)
    live_y = lax.dynamic_index_in_dim(live_y, y, 2, keepdims=False)[:, :, 2:]
    order_z = (z - jnp.arange(n_z, dtype=jnp.int32)) % n_z
    live_y = jnp.take(live_y, order_z, axis=1).reshape(-1)
    part_z = attend(
        live_y, from_y, along_z, (n_y, n_grp, 16, 128), (1, n_grp, 16, 128), lambda u: (u, 0, 0, 0), "attend_along_z"
    )
    shared = jnp.sum(exchange(part_z, "yl").astype(jnp.float32), axis=0)

    live_z = from_z[:, PIECE].astype(jnp.int32).reshape(n_z, n_z, n_y, 4)
    live_z = lax.dynamic_index_in_dim(live_z, z, 1, keepdims=False)[:, :, :2]
    order_y = y ^ jnp.arange(n_y, dtype=jnp.int32)
    live_z = jnp.take(live_z, order_y, axis=1).reshape(-1)
    part_y = attend(
        live_z, from_z, along_y, (n_grp, n_z, 16, 128), (n_grp, 1, 16, 128), lambda u: (0, u, 0, 0), "attend_along_y"
    )
    mine = (jnp.arange(n_z, dtype=jnp.int32) == z)[None, :, None, None]
    partial = (part_y.astype(jnp.float32) + jnp.where(mine, shared[:, None], 0.0)).astype(jnp.bfloat16)
    parts = exchange(partial.reshape(n_grp * n_z, 16, 128), GRP + ("z",)).reshape(n_grp, n_z, 16, 128)
    keep = cand_count - lax.axis_index(GRP) * own_rows
    return output(keep, parts, gates, w_full, rows).reshape(cand_x.shape)


def solution(mesh):
    split = Mesh(mesh.devices.reshape(2, 4, 2, 8, 4), ("yh", "x", "c", "z", "yl"))
    hist = ("z", "yl")
    in_specs = (
        P(GRP, hist, None),
        P(None, hist, GRP),
        P(hist),
        P(hist),
        P(hist, None),
        P(None, GRP),
        P(GRP, None),
    )
    return jax.shard_map(
        functools.partial(per_device, (16, 8, 4)),
        mesh=split,
        in_specs=in_specs,
        out_specs=P(GRP, hist, None),
        check_vma=False,
    )
```

```python
import functools

import jax
import jax.numpy as jnp
from jax import lax
from jax.experimental import pallas as pl
from jax.experimental.pallas import tpu as pltpu
from jax.sharding import Mesh
from jax.sharding import PartitionSpec as P

D = 1024
BLK = 128
TILE = 2048
CHUNKS = ((0, 256), (256, 384), (384, 512))
GRP = ("yh", "x", "c")
HALF = 64
PARAMS = pltpu.CompilerParams(vmem_limit_bytes=24 * 1024 * 1024)


def layer_norm(values):
    average = jnp.mean(values, axis=-1, keepdims=True)
    centred = values - average
    spread = jnp.mean(centred * centred, axis=-1, keepdims=True)
    return centred * lax.rsqrt(spread + 1e-05)


def low_lanes(shape):
    return lax.broadcasted_iota(jnp.int32, shape, len(shape) - 1) < HALF


def member(place_ref, turns, core, half):
    yh, x, c = place_ref[0], place_ref[1], place_ref[2]
    return (yh ^ half) * 8 + lax.rem(x - turns + 4, 4) * 2 + (c ^ core)


def project_kernel(place_ref, *refs):
    quads, (w_ref, query_ref, gate_ref) = refs[:4], refs[4:]
    for turns, quad in enumerate(quads):
        _, _, own, width = quad.shape
        rows = quad[...].reshape(4 * own, width).astype(jnp.float32)
        normed = layer_norm(rows).astype(jnp.bfloat16)
        product = jnp.dot(normed, w_ref[...], preferred_element_type=jnp.float32)
        values = (product / (1.0 + jnp.exp(-product))).astype(jnp.bfloat16).astype(jnp.float32)
        query = jnp.where(low_lanes(values.shape), values * (0.5 * HALF ** (-0.5)), 0.0).astype(jnp.bfloat16)
        pairs = values.reshape(4, 2, own // 2, 128)
        first, second = pairs[:, 0], pairs[:, 1]
        turned = pltpu.roll(first.reshape(-1, 128), HALF, 1).reshape(first.shape)
        gate = jnp.where(low_lanes(first.shape), turned, second).astype(jnp.bfloat16)
        for core in range(2):
            for half in range(2):
                at = member(place_ref, turns, core, half)
                block = core * 2 + half
                query_ref[pl.ds(pl.multiple_of(at * own, own), own)] = query[block * own : (block + 1) * own]
                gate_ref[at] = gate[block]


def project(place, quads, w_proj):
    own = quads[0].shape[2]
    vmem = pl.BlockSpec(memory_space=pltpu.VMEM)
    return pl.pallas_call(
        project_kernel,
        out_shape=(
            jax.ShapeDtypeStruct((16 * own, 128), jnp.bfloat16),
            jax.ShapeDtypeStruct((16, own // 2, 128), jnp.bfloat16),
        ),
        in_specs=[pl.BlockSpec(memory_space=pltpu.SMEM)] + [vmem] * 5,
        out_specs=(vmem, vmem),
        compiler_params=PARAMS,
        cost_estimate=pl.CostEstimate(flops=2 * 512 * D * 128, bytes_accessed=2 << 20, transcendentals=0),
        name="project",
    )(place, *quads, w_proj)


def attend_tiles(live_ref, count_ref, query_ref, kv_ref, total, masked):
    step = pl.program_id(0)
    blocks = kv_ref.shape[0] // BLK
    lives = [live_ref[step * blocks + i] for i in range(blocks)]

    @pl.when(functools.reduce(jnp.add, lives) > 0)
    def _():
        row = lax.broadcasted_iota(jnp.int32, (BLK, 128), 0)
        for i in range(blocks):
            block = kv_ref[i * BLK : (i + 1) * BLK]
            masked[i * BLK : (i + 1) * BLK] = jnp.where(row < lives[i], block, jnp.zeros_like(block))
        for start, end in CHUNKS:

            @pl.when(count_ref[0] > start)
            def _():
                scores = lax.dot_general(
                    query_ref[start:end], masked[...], (((1,), (1,)), ((), ())), preferred_element_type=jnp.float32
                )
                weights = (scores + scores * jnp.tanh(scores)).astype(jnp.bfloat16)
                total[start:end] += jnp.dot(weights, masked[...], preferred_element_type=jnp.float32)


def attend_first_kernel(live_ref, count_ref, query_ref, kv_ref, total, masked):
    @pl.when(pl.program_id(0) == 0)
    def _():
        total[...] = jnp.zeros_like(total)

    attend_tiles(live_ref, count_ref, query_ref, kv_ref, total, masked)


def attend_last_kernel(live_ref, count_ref, query_ref, kv_ref, before_ref, gate_ref, out_ref, total, masked):
    @pl.when(pl.program_id(0) == 0)
    def _():
        total[...] = before_ref[...]

    attend_tiles(live_ref, count_ref, query_ref, kv_ref, total, masked)

    @pl.when(pl.program_id(0) == pl.num_programs(0) - 1)
    def _():
        slices = total[...].reshape(out_ref.shape[0], 2, 16, 128)
        first, second = slices[:, 0], slices[:, 1]
        turned = pltpu.roll(first.reshape(-1, 128), HALF, 1).reshape(first.shape)
        out_ref[:, 0:16, :] = jnp.where(low_lanes(first.shape), turned, second).astype(jnp.bfloat16)
        out_ref[:, 16:32, :] = gate_ref[...]


def attend(live, cand_count, query, kv, before=None, gate=None):
    count = query.shape[0]
    positions = kv.shape[0]
    smem = pl.BlockSpec(memory_space=pltpu.SMEM)
    in_specs = [smem, smem, pl.BlockSpec((count, 128), lambda i: (0, 0)), pl.BlockSpec((TILE, 128), lambda i: (i, 0))]
    masked = pltpu.VMEM((TILE, 128), jnp.bfloat16)
    running = pltpu.VMEM((count, 128), jnp.float32)
    common = dict(
        grid=(positions // TILE,),
        compiler_params=PARAMS,
        cost_estimate=pl.CostEstimate(
            flops=4 * count * positions * 128, bytes_accessed=positions * 256, transcendentals=count * positions
        ),
    )
    if before is None:
        return pl.pallas_call(
            attend_first_kernel,
            out_shape=jax.ShapeDtypeStruct((count, 128), jnp.float32),
            in_specs=in_specs,
            out_specs=pl.BlockSpec((count, 128), lambda i: (0, 0)),
            scratch_shapes=[masked],
            name="attend_first",
            **common,
        )(live, cand_count, query, kv)
    return pl.pallas_call(
        attend_last_kernel,
        out_shape=jax.ShapeDtypeStruct((count // 32, 32, 128), jnp.bfloat16),
        in_specs=in_specs
        + [pl.BlockSpec((count, 128), lambda i: (0, 0)), pl.BlockSpec((count // 32, 16, 128), lambda i: (0, 0, 0))],
        out_specs=pl.BlockSpec((count // 32, 32, 128), lambda i: (0, 0, 0)),
        scratch_shapes=[running, masked],
        name="attend_last",
        **common,
    )(live, cand_count, query, kv, before, gate)


def spread_heads(packed):
    columns = []
    for pair in range(len(packed) // 2):
        even, odd = packed[2 * pair], packed[2 * pair + 1]
        low = low_lanes(even.shape)
        top = jnp.where(low, even, pltpu.roll(odd, HALF, 1))
        bottom = jnp.where(low, pltpu.roll(even, HALF, 1), odd)
        columns.append(jnp.concatenate([top, bottom], axis=0))
    return jnp.concatenate(columns, axis=1)


def output_kernel(place_ref, count_ref, parts_ref, *refs):
    quads, (x_ref, out_ref) = refs[:4], refs[4:]
    attended, gate = [], []
    for turns in range(4):
        for core in range(2):
            for half in range(2):
                part = parts_ref[member(place_ref, turns, core, half)].astype(jnp.float32)
                attended.append(part[0:16])
                gate.append(part[16:32])
    gated = (layer_norm(spread_heads(attended)) * spread_heads(gate)).astype(jnp.bfloat16)
    mixed = x_ref[...].astype(jnp.float32)
    for turns, quad in enumerate(quads):
        depth = 4 * quad.shape[2]
        weights = quad[...].reshape(depth, quad.shape[3])
        mixed += jnp.dot(gated[:, turns * depth : (turns + 1) * depth], weights, preferred_element_type=jnp.float32)
    row = lax.broadcasted_iota(jnp.int32, mixed.shape, 0)
    out_ref[...] = jnp.where(row < count_ref[0], mixed, 0.0).astype(jnp.bfloat16)


def output(place, keep, parts, quads, rows):
    smem, vmem = pl.BlockSpec(memory_space=pltpu.SMEM), pl.BlockSpec(memory_space=pltpu.VMEM)
    return pl.pallas_call(
        output_kernel,
        out_shape=jax.ShapeDtypeStruct(rows.shape, jnp.bfloat16),
        in_specs=[smem, smem] + [vmem] * 6,
        out_specs=vmem,
        compiler_params=PARAMS,
        cost_estimate=pl.CostEstimate(flops=2 * 32 * D * D, bytes_accessed=3 << 20, transcendentals=0),
        name="output",
    )(place, keep, parts, *quads, rows)


def exchange(values, axes):
    return lax.all_to_all(values, axes, split_axis=0, concat_axis=0, tiled=True)


def swap(values, axis):
    return lax.ppermute(values, axis, [(0, 1), (1, 0)])


def go_round(pair):
    quad = jnp.stack([pair, swap(pair, "c")])
    return [quad] + [lax.ppermute(quad, "x", [(i, (i + turns) % 4) for i in range(4)]) for turns in (1, 2, 3)]


def per_device(cand_x, hist_kv, hist_len, cand_count, block_mask, w_proj, w_out):
    own_rows = cand_x.shape[0]
    rows = cand_x.reshape(own_rows, D)
    place = jnp.stack([lax.axis_index("yh"), lax.axis_index("x"), lax.axis_index("c")]).astype(jnp.int32)
    other_rows, other_w = swap(rows, "yh"), swap(w_out, "yh")
    hist_kv, other_rows, other_w = lax.optimization_barrier((hist_kv, other_rows, other_w))
    hist = ("z", "yl")
    bulk = exchange(hist_kv[:, 2 * BLK :], hist)
    bulk, hist_kv, other_rows, other_w = lax.optimization_barrier((bulk, hist_kv, other_rows, other_w))
    rest = exchange(hist_kv[:, : 2 * BLK], hist)

    starts = jnp.arange(block_mask.shape[1], dtype=jnp.int32) * BLK
    live = (jnp.clip(hist_len[0] - starts, 0, BLK) * block_mask[0]).reshape(-1, 4)
    query, gate = project(place, go_round(jnp.stack([rows, other_rows])), w_proj)
    total = attend(live[:, 2:].reshape(-1), cand_count, query, bulk.reshape(-1, 128))
    w_quads = go_round(jnp.stack([w_out, other_w]))
    attended = attend(live[:, :2].reshape(-1), cand_count, query, rest.reshape(-1, 128), total, gate)
    attended, *w_quads = lax.optimization_barrier((attended, *w_quads))
    parts = exchange(attended, GRP)
    keep = cand_count - lax.axis_index(GRP) * own_rows
    return output(place, keep, parts, w_quads, rows).reshape(cand_x.shape)


def solution(mesh):
    split = Mesh(mesh.devices.reshape(2, 4, 2, 8, 4), ("yh", "x", "c", "z", "yl"))
    hist = ("z", "yl")
    in_specs = (
        P(GRP, hist, None),
        P(None, hist, GRP),
        P(hist),
        P(hist),
        P(hist, None),
        P(None, GRP),
        P(GRP, None),
    )
    return jax.shard_map(per_device, mesh=split, in_specs=in_specs, out_specs=P(GRP, hist, None), check_vma=False)
```

```python
import functools

import jax
import jax.numpy as jnp
from jax import lax
from jax.experimental import pallas as pl
from jax.experimental.pallas import tpu as pltpu
from jax.sharding import Mesh
from jax.sharding import PartitionSpec as P

D = 1024
BLK = 128
FINE = 128
FIRST = 256
GRP = ("yh", "x", "c")
HALF = 64
PARAMS = pltpu.CompilerParams(vmem_limit_bytes=24 * 1024 * 1024)


def layer_norm(values):
    average = jnp.mean(values, axis=-1, keepdims=True)
    centred = values - average
    spread = jnp.mean(centred * centred, axis=-1, keepdims=True)
    return centred * lax.rsqrt(spread + 1e-05)


def low_lanes(shape):
    return lax.broadcasted_iota(jnp.int32, shape, len(shape) - 1) < HALF


def member(place_ref, turns, core, half):
    yh, x, c = place_ref[0], place_ref[1], place_ref[2]
    return (yh ^ half) * 8 + lax.rem(x - turns + 4, 4) * 2 + (c ^ core)


def project_kernel(place_ref, *refs):
    quads, (w_ref, query_ref, gate_ref) = refs[:4], refs[4:]
    for turns, quad in enumerate(quads):
        _, _, own, width = quad.shape
        rows = quad[...].reshape(4 * own, width).astype(jnp.float32)
        normed = layer_norm(rows).astype(jnp.bfloat16)
        product = jnp.dot(normed, w_ref[...], preferred_element_type=jnp.float32)
        values = (product / (1.0 + jnp.exp(-product))).astype(jnp.bfloat16).astype(jnp.float32)
        query = jnp.where(low_lanes(values.shape), values * (0.5 * HALF ** (-0.5)), 0.0).astype(jnp.bfloat16)
        pairs = values.reshape(4, 2, own // 2, 128)
        first, second = pairs[:, 0], pairs[:, 1]
        turned = pltpu.roll(first.reshape(-1, 128), HALF, 1).reshape(first.shape)
        gate = jnp.where(low_lanes(first.shape), turned, second).astype(jnp.bfloat16)
        for core in range(2):
            for half in range(2):
                at = member(place_ref, turns, core, half)
                block = core * 2 + half
                query_ref[pl.ds(pl.multiple_of(at * own, own), own)] = query[block * own : (block + 1) * own]
                gate_ref[at] = gate[block]


def project(place, quads, w_proj):
    own = quads[0].shape[2]
    vmem = pl.BlockSpec(memory_space=pltpu.VMEM)
    return pl.pallas_call(
        project_kernel,
        out_shape=(
            jax.ShapeDtypeStruct((16 * own, 128), jnp.bfloat16),
            jax.ShapeDtypeStruct((16, own // 2, 128), jnp.bfloat16),
        ),
        in_specs=[pl.BlockSpec(memory_space=pltpu.SMEM)] + [vmem] * 5,
        out_specs=(vmem, vmem),
        compiler_params=PARAMS,
        cost_estimate=pl.CostEstimate(flops=2 * 512 * D * 128, bytes_accessed=2 << 20, transcendentals=0),
        name="project",
    )(place, *quads, w_proj)


def attend_tiles(offset, length_ref, mask_ref, count_ref, query_ref, kv_ref, total, masked):
    step = pl.program_id(0)
    sources, rows, _ = kv_ref.shape
    lives = []
    for source in range(sources):
        for block in range(rows // FINE):
            position = (step * sources + source) * 512 + offset + block * FINE
            count = jnp.clip(length_ref[0] - position, 0, FINE)
            lives.append(count * mask_ref[0, (step * sources + source) * 4 + (offset + block * FINE) // BLK])

    def attend_rows(chunks):
        row = lax.broadcasted_iota(jnp.int32, (FINE, 128), 0)
        for i, live in enumerate(lives):
            source, block = divmod(i, rows // FINE)
            piece = kv_ref[source, block * FINE : (block + 1) * FINE]
            masked[i * FINE : (i + 1) * FINE] = jnp.where(row < live, piece, jnp.zeros_like(piece))
        for start, end in chunks:
            scores = lax.dot_general(
                query_ref[start:end], masked[...], (((1,), (1,)), ((), ())), preferred_element_type=jnp.float32
            )
            weights = (scores + scores * jnp.tanh(scores)).astype(jnp.bfloat16)
            total[start:end] += jnp.dot(weights, masked[...], preferred_element_type=jnp.float32)

    some = functools.reduce(jnp.add, lives) > 0
    few = count_ref[0] <= 384

    @pl.when(jnp.logical_and(some, few))
    def _():
        attend_rows(((0, 256), (256, 384)))

    @pl.when(jnp.logical_and(some, jnp.logical_not(few)))
    def _():
        attend_rows(((0, 256), (256, 512)))


def attend_first_kernel(offset, length_ref, mask_ref, count_ref, query_ref, kv_ref, total, masked):
    @pl.when(pl.program_id(0) == 0)
    def _():
        total[...] = jnp.zeros_like(total)

    attend_tiles(offset, length_ref, mask_ref, count_ref, query_ref, kv_ref, total, masked)


def attend_last_kernel(
    offset, length_ref, mask_ref, count_ref, query_ref, kv_ref, before_ref, gate_ref, out_ref, total, masked
):
    @pl.when(pl.program_id(0) == 0)
    def _():
        total[...] = before_ref[...]

    attend_tiles(offset, length_ref, mask_ref, count_ref, query_ref, kv_ref, total, masked)

    @pl.when(pl.program_id(0) == pl.num_programs(0) - 1)
    def _():
        slices = total[...].reshape(out_ref.shape[0], 2, 16, 128)
        first, second = slices[:, 0], slices[:, 1]
        turned = pltpu.roll(first.reshape(-1, 128), HALF, 1).reshape(first.shape)
        packed = jnp.where(low_lanes(first.shape), turned, second)
        high = packed.astype(jnp.bfloat16)
        out_ref[:, 0:16, :] = high
        out_ref[:, 16:32, :] = (packed - high.astype(jnp.float32)).astype(jnp.bfloat16)
        out_ref[:, 32:48, :] = gate_ref[...]


def attend(offset, sources, length, mask, cand_count, query, kv, before=None, gate=None):
    count = query.shape[0]
    devices, rows, _ = kv.shape
    smem = pl.BlockSpec(memory_space=pltpu.SMEM)
    in_specs = [
        smem,
        smem,
        smem,
        pl.BlockSpec((count, 128), lambda i: (0, 0)),
        pl.BlockSpec((sources, rows, 128), lambda i: (i, 0, 0)),
    ]
    masked = pltpu.VMEM((sources * rows, 128), jnp.bfloat16)
    running = pltpu.VMEM((count, 128), jnp.float32)
    positions = devices * rows
    common = dict(
        grid=(devices // sources,),
        compiler_params=PARAMS,
        cost_estimate=pl.CostEstimate(
            flops=4 * count * positions * 128, bytes_accessed=positions * 256, transcendentals=count * positions
        ),
    )
    if before is None:
        return pl.pallas_call(
            functools.partial(attend_first_kernel, offset),
            out_shape=jax.ShapeDtypeStruct((count, 128), jnp.float32),
            in_specs=in_specs,
            out_specs=pl.BlockSpec((count, 128), lambda i: (0, 0)),
            scratch_shapes=[masked],
            name="attend_first",
            **common,
        )(length, mask, cand_count, query, kv)
    return pl.pallas_call(
        functools.partial(attend_last_kernel, offset),
        out_shape=jax.ShapeDtypeStruct((count // 32, 48, 128), jnp.bfloat16),
        in_specs=in_specs
        + [pl.BlockSpec((count, 128), lambda i: (0, 0)), pl.BlockSpec((count // 32, 16, 128), lambda i: (0, 0, 0))],
        out_specs=pl.BlockSpec((count // 32, 48, 128), lambda i: (0, 0, 0)),
        scratch_shapes=[running, masked],
        name="attend_last",
        **common,
    )(length, mask, cand_count, query, kv, before, gate)


def spread_heads(packed):
    columns = []
    for pair in range(len(packed) // 2):
        even, odd = packed[2 * pair], packed[2 * pair + 1]
        low = low_lanes(even.shape)
        top = jnp.where(low, even, pltpu.roll(odd, HALF, 1))
        bottom = jnp.where(low, pltpu.roll(even, HALF, 1), odd)
        columns.append(jnp.concatenate([top, bottom], axis=0))
    return jnp.concatenate(columns, axis=1)


def output_kernel(place_ref, count_ref, parts_ref, *refs):
    quads, (x_ref, out_ref) = refs[:4], refs[4:]
    attended, gate = [], []
    for turns in range(4):
        for core in range(2):
            for half in range(2):
                part = parts_ref[member(place_ref, turns, core, half)].astype(jnp.float32)
                attended.append(part[0:16] + part[16:32])
                gate.append(part[32:48])
    gated = (layer_norm(spread_heads(attended)) * spread_heads(gate)).astype(jnp.bfloat16)
    mixed = x_ref[...].astype(jnp.float32)
    for turns, quad in enumerate(quads):
        depth = 4 * quad.shape[2]
        weights = quad[...].reshape(depth, quad.shape[3])
        mixed += jnp.dot(gated[:, turns * depth : (turns + 1) * depth], weights, preferred_element_type=jnp.float32)
    row = lax.broadcasted_iota(jnp.int32, mixed.shape, 0)
    out_ref[...] = jnp.where(row < count_ref[0], mixed, 0.0).astype(jnp.bfloat16)


def output(place, keep, parts, quads, rows):
    smem, vmem = pl.BlockSpec(memory_space=pltpu.SMEM), pl.BlockSpec(memory_space=pltpu.VMEM)
    return pl.pallas_call(
        output_kernel,
        out_shape=jax.ShapeDtypeStruct(rows.shape, jnp.bfloat16),
        in_specs=[smem, smem] + [vmem] * 6,
        out_specs=vmem,
        compiler_params=PARAMS,
        cost_estimate=pl.CostEstimate(flops=2 * 32 * D * D, bytes_accessed=3 << 20, transcendentals=0),
        name="output",
    )(place, keep, parts, *quads, rows)


def exchange(values, axes):
    return lax.all_to_all(values, axes, split_axis=0, concat_axis=0, tiled=True)


def swap(values, axis):
    return lax.ppermute(values, axis, [(0, 1), (1, 0)])


def go_round(pair):
    quad = jnp.stack([pair, swap(pair, "c")])
    return [quad] + [lax.ppermute(quad, "x", [(i, (i + turns) % 4) for i in range(4)]) for turns in (1, 2, 3)]


def per_device(cand_x, hist_kv, hist_len, cand_count, block_mask, w_proj, w_out):
    own_rows = cand_x.shape[0]
    rows = cand_x.reshape(own_rows, D)
    place = jnp.stack([lax.axis_index("yh"), lax.axis_index("x"), lax.axis_index("c")]).astype(jnp.int32)
    other_rows, other_w = swap(rows, "yh"), swap(w_out, "yh")
    first, second, other_rows, other_w = lax.optimization_barrier(
        (hist_kv[:, :FIRST], hist_kv[:, FIRST:], other_rows, other_w)
    )
    hist = ("z", "yl")
    bulk = exchange(first, hist)
    bulk, second, other_rows, other_w = lax.optimization_barrier((bulk, second, other_rows, other_w))
    rest = exchange(second, hist)

    limits = (hist_len, block_mask, cand_count)
    query, gate = project(place, go_round(jnp.stack([rows, other_rows])), w_proj)
    total = attend(0, 8, *limits, query, bulk)
    w_quads = go_round(jnp.stack([w_out, other_w]))
    attended = attend(FIRST, 8, *limits, query, rest, total, gate)
    keep = cand_count - lax.axis_index(GRP) * own_rows
    parts = exchange(attended, GRP)
    return output(place, keep, parts, w_quads, rows).reshape(cand_x.shape)


def solution(mesh):
    split = Mesh(mesh.devices.reshape(2, 4, 2, 8, 4), ("yh", "x", "c", "z", "yl"))
    hist = ("z", "yl")
    in_specs = (
        P(GRP, hist, None),
        P(None, hist, GRP),
        P(hist),
        P(hist),
        P(hist, None),
        P(None, GRP),
        P(GRP, None),
    )
    return jax.shard_map(per_device, mesh=split, in_specs=in_specs, out_specs=P(GRP, hist, None), check_vma=False)
```

```python
import functools

import jax
import jax.numpy as jnp
from jax import lax
from jax.experimental import pallas as pl
from jax.experimental.pallas import tpu as pltpu
from jax.sharding import Mesh
from jax.sharding import PartitionSpec as P

D = 1024
BLK = 128
FINE = 64
FIRST = 320
GRP = ("yh", "x", "c")
HALF = 64
PARAMS = pltpu.CompilerParams(vmem_limit_bytes=24 * 1024 * 1024)


def layer_norm(values):
    average = jnp.mean(values, axis=-1, keepdims=True)
    centred = values - average
    spread = jnp.mean(centred * centred, axis=-1, keepdims=True)
    return centred * lax.rsqrt(spread + 1e-05)


def low_lanes(shape):
    return lax.broadcasted_iota(jnp.int32, shape, len(shape) - 1) < HALF


def member(place_ref, turns, core, half):
    yh, x, c = place_ref[0], place_ref[1], place_ref[2]
    return (yh ^ half) * 8 + lax.rem(x - turns + 4, 4) * 2 + (c ^ core)


def project_kernel(place_ref, length_ref, mask_ref, *refs):
    quads, (w_ref, query_ref, gate_ref, message_ref) = refs[:4], refs[4:]
    block = lax.broadcasted_iota(jnp.int32, (16, 128), 1)
    live = jnp.clip(length_ref[0] - block * BLK, 0, BLK) * mask_ref[...]
    message_ref[256:272] = live.astype(jnp.float32).astype(jnp.bfloat16)
    for turns, quad in enumerate(quads):
        _, _, own, width = quad.shape
        rows = quad[...].reshape(4 * own, width).astype(jnp.float32)
        normed = layer_norm(rows).astype(jnp.bfloat16)
        product = jnp.dot(normed, w_ref[...], preferred_element_type=jnp.float32)
        values = (product / (1.0 + jnp.exp(-product))).astype(jnp.bfloat16).astype(jnp.float32)
        query = jnp.where(low_lanes(values.shape), values * (0.5 * HALF ** (-0.5)), 0.0).astype(jnp.bfloat16)
        pairs = values.reshape(4, 2, own // 2, 128)
        first, second = pairs[:, 0], pairs[:, 1]
        turned = pltpu.roll(first.reshape(-1, 128), HALF, 1).reshape(first.shape)
        gate = jnp.where(low_lanes(first.shape), turned, second).astype(jnp.bfloat16)
        turned = pltpu.roll(second.reshape(-1, 128), HALF, 1).reshape(second.shape)
        packed = (jnp.where(low_lanes(first.shape), first, turned) * (0.5 * HALF ** (-0.5))).astype(jnp.bfloat16)
        for core in range(2):
            for half in range(2):
                at = member(place_ref, turns, core, half)
                block = core * 2 + half
                query_ref[pl.ds(pl.multiple_of(at * own, own), own)] = query[block * own : (block + 1) * own]
                gate_ref[at] = gate[block]
                message_ref[pl.ds(pl.multiple_of(at * 16, 16), 16)] = packed[block]


def project(place, length, mask, quads, w_proj):
    own = quads[0].shape[2]
    vmem = pl.BlockSpec(memory_space=pltpu.VMEM)
    return pl.pallas_call(
        project_kernel,
        out_shape=(
            jax.ShapeDtypeStruct((16 * own, 128), jnp.bfloat16),
            jax.ShapeDtypeStruct((16, own // 2, 128), jnp.bfloat16),
            jax.ShapeDtypeStruct((272, 128), jnp.bfloat16),
        ),
        in_specs=[pl.BlockSpec(memory_space=pltpu.SMEM)] * 2 + [vmem] * 6,
        out_specs=(vmem, vmem, vmem),
        compiler_params=PARAMS,
        cost_estimate=pl.CostEstimate(flops=2 * 512 * D * 128, bytes_accessed=2 << 20, transcendentals=0),
        name="project",
    )(place, length, mask, *quads, w_proj)


def attend_tiles(offset, length_ref, mask_ref, count_ref, query_ref, kv_ref, total, masked):
    step = pl.program_id(0)
    sources, rows, _ = kv_ref.shape
    lives = []
    for source in range(sources):
        for block in range(rows // FINE):
            position = (step * sources + source) * 512 + offset + block * FINE
            count = jnp.clip(length_ref[0] - position, 0, FINE)
            lives.append(count * mask_ref[0, (step * sources + source) * 4 + (offset + block * FINE) // BLK])

    def attend_rows(chunks):
        row = lax.broadcasted_iota(jnp.int32, (FINE, 128), 0)
        for i, live in enumerate(lives):
            source, block = divmod(i, rows // FINE)
            piece = kv_ref[source, block * FINE : (block + 1) * FINE]
            masked[i * FINE : (i + 1) * FINE] = jnp.where(row < live, piece, jnp.zeros_like(piece))
        for start, end in chunks:
            scores = lax.dot_general(
                query_ref[start:end], masked[...], (((1,), (1,)), ((), ())), preferred_element_type=jnp.float32
            )
            weights = (scores + scores * jnp.tanh(scores)).astype(jnp.bfloat16)
            total[start:end] += jnp.dot(weights, masked[...], preferred_element_type=jnp.float32)

    some = functools.reduce(jnp.add, lives) > 0
    few = count_ref[0] <= 384

    @pl.when(jnp.logical_and(some, few))
    def _():
        attend_rows(((0, 256), (256, 384)))

    @pl.when(jnp.logical_and(some, jnp.logical_not(few)))
    def _():
        attend_rows(((0, 256), (256, 512)))


def attend_plane_kernel(y_ref, live_ref, message_ref, kv_ref, out_ref, masked):
    user = pl.program_id(0)
    planes, _, rows, _ = kv_ref.shape
    pieces = rows // FINE
    blocks = -(-rows // BLK)
    lives = []
    for plane in range(planes):
        for piece in range(pieces):
            block, part = divmod(piece * FINE, BLK)
            lives.append(jnp.clip(live_ref[(user * planes + plane) * blocks + block] - part, 0, FINE))
    some = functools.reduce(jnp.add, lives) > 0

    @pl.when(some)
    def _():
        row = lax.broadcasted_iota(jnp.int32, (FINE, 128), 0)
        for i, live in enumerate(lives):
            plane, piece = divmod(i, pieces)
            values = kv_ref[plane, 0, piece * FINE : (piece + 1) * FINE]
            masked[i * FINE : (i + 1) * FINE] = jnp.where(row < live, values, jnp.zeros_like(values))
        packed = message_ref[0, 0:256].astype(jnp.float32)
        low = low_lanes(packed.shape)
        totals = []
        for values in (packed, pltpu.roll(packed, HALF, 1)):
            query = jnp.where(low, values, 0.0).astype(jnp.bfloat16)
            scores = lax.dot_general(
                query, masked[...], (((1,), (1,)), ((), ())), preferred_element_type=jnp.float32
            )
            weights = (scores + scores * jnp.tanh(scores)).astype(jnp.bfloat16)
            totals.append(jnp.dot(weights, masked[...], preferred_element_type=jnp.float32))
        out_ref[0] = jnp.where(low, pltpu.roll(totals[0], HALF, 1), totals[1])

    @pl.when(jnp.logical_not(some))
    def _():
        out_ref[...] = jnp.zeros_like(out_ref)


def attend_plane(y, live, messages, kv):
    planes, users, rows, _ = kv.shape
    return pl.pallas_call(
        attend_plane_kernel,
        out_shape=jax.ShapeDtypeStruct((users, 256, 128), jnp.float32),
        grid_spec=pltpu.PrefetchScalarGridSpec(
            num_scalar_prefetch=1,
            grid=(users,),
            in_specs=[
                pl.BlockSpec(memory_space=pltpu.SMEM),
                pl.BlockSpec((1, 272, 128), lambda i, y: (i, 0, 0)),
                pl.BlockSpec((planes, 1, rows, 128), lambda i, y: (0, y[0] ^ i, 0, 0)),
            ],
            out_specs=pl.BlockSpec((1, 256, 128), lambda i, y: (i, 0, 0)),
            scratch_shapes=[pltpu.VMEM((planes * rows, 128), jnp.bfloat16)],
        ),
        compiler_params=PARAMS,
        cost_estimate=pl.CostEstimate(flops=1 << 30, bytes_accessed=3 << 20, transcendentals=1 << 22),
        name="attend_plane",
    )(y, live, messages, kv)


def attend_last_kernel(
    offset, length_ref, mask_ref, count_ref, query_ref, kv_ref, gate_ref, a_ref, b_ref, c_ref, d_ref, out_ref, total, masked
):
    @pl.when(pl.program_id(0) == 0)
    def _():
        total[...] = jnp.zeros_like(total)

    attend_tiles(offset, length_ref, mask_ref, count_ref, query_ref, kv_ref, total, masked)

    @pl.when(pl.program_id(0) == pl.num_programs(0) - 1)
    def _():
        slices = total[...].reshape(out_ref.shape[0], 2, 16, 128)
        first, second = slices[:, 0], slices[:, 1]
        turned = pltpu.roll(first.reshape(-1, 128), HALF, 1).reshape(first.shape)
        packed = jnp.where(low_lanes(first.shape), turned, second)
        others = a_ref[...] + b_ref[...] + c_ref[...] + d_ref[...]
        packed += others.reshape(packed.shape)
        high = packed.astype(jnp.bfloat16)
        out_ref[:, 0:16, :] = high
        out_ref[:, 16:32, :] = (packed - high.astype(jnp.float32)).astype(jnp.bfloat16)
        out_ref[:, 32:48, :] = gate_ref[...]


def attend_last(offset, sources, length, mask, cand_count, query, kv, gate, sums):
    count = query.shape[0]
    devices, rows, _ = kv.shape
    smem = pl.BlockSpec(memory_space=pltpu.SMEM)
    positions = devices * rows
    return pl.pallas_call(
        functools.partial(attend_last_kernel, offset),
        out_shape=jax.ShapeDtypeStruct((count // 32, 48, 128), jnp.bfloat16),
        grid=(devices // sources,),
        in_specs=[
            smem,
            smem,
            smem,
            pl.BlockSpec((count, 128), lambda i: (0, 0)),
            pl.BlockSpec((sources, rows, 128), lambda i: (i, 0, 0)),
            pl.BlockSpec((count // 32, 16, 128), lambda i: (0, 0, 0)),
        ]
        + [pl.BlockSpec((256, 128), lambda i: (0, 0))] * 4,
        out_specs=pl.BlockSpec((count // 32, 48, 128), lambda i: (0, 0, 0)),
        scratch_shapes=[pltpu.VMEM((count, 128), jnp.float32), pltpu.VMEM((sources * rows, 128), jnp.bfloat16)],
        compiler_params=PARAMS,
        cost_estimate=pl.CostEstimate(
            flops=4 * count * positions * 128, bytes_accessed=positions * 256, transcendentals=count * positions
        ),
        name="attend_last",
    )(length, mask, cand_count, query, kv, gate, *sums)


def spread_heads(packed):
    columns = []
    for pair in range(len(packed) // 2):
        even, odd = packed[2 * pair], packed[2 * pair + 1]
        low = low_lanes(even.shape)
        top = jnp.where(low, even, pltpu.roll(odd, HALF, 1))
        bottom = jnp.where(low, pltpu.roll(even, HALF, 1), odd)
        columns.append(jnp.concatenate([top, bottom], axis=0))
    return jnp.concatenate(columns, axis=1)


def output_kernel(place_ref, count_ref, parts_ref, *refs):
    quads, (x_ref, out_ref) = refs[:4], refs[4:]
    attended, gate = [], []
    for turns in range(4):
        for core in range(2):
            for half in range(2):
                part = parts_ref[member(place_ref, turns, core, half)].astype(jnp.float32)
                attended.append(part[0:16] + part[16:32])
                gate.append(part[32:48])
    gated = (layer_norm(spread_heads(attended)) * spread_heads(gate)).astype(jnp.bfloat16)
    mixed = x_ref[...].astype(jnp.float32)
    for turns, quad in enumerate(quads):
        depth = 4 * quad.shape[2]
        weights = quad[...].reshape(depth, quad.shape[3])
        mixed += jnp.dot(gated[:, turns * depth : (turns + 1) * depth], weights, preferred_element_type=jnp.float32)
    row = lax.broadcasted_iota(jnp.int32, mixed.shape, 0)
    out_ref[...] = jnp.where(row < count_ref[0], mixed, 0.0).astype(jnp.bfloat16)


def output(place, keep, parts, quads, rows):
    smem, vmem = pl.BlockSpec(memory_space=pltpu.SMEM), pl.BlockSpec(memory_space=pltpu.VMEM)
    return pl.pallas_call(
        output_kernel,
        out_shape=jax.ShapeDtypeStruct(rows.shape, jnp.bfloat16),
        in_specs=[smem, smem] + [vmem] * 6,
        out_specs=vmem,
        compiler_params=PARAMS,
        cost_estimate=pl.CostEstimate(flops=2 * 32 * D * D, bytes_accessed=3 << 20, transcendentals=0),
        name="output",
    )(place, keep, parts, *quads, rows)


def exchange(values, axes):
    return lax.all_to_all(values, axes, split_axis=0, concat_axis=0, tiled=True)


def swap(values, axis):
    return lax.ppermute(values, axis, [(0, 1), (1, 0)])


def go_round(pair):
    quad = jnp.stack([pair, swap(pair, "c")])
    return [quad] + [lax.ppermute(quad, "x", [(i, (i + turns) % 4) for i in range(4)]) for turns in (1, 2, 3)]


def per_device(cand_x, hist_kv, hist_len, cand_count, block_mask, w_proj, w_out):
    own_rows = cand_x.shape[0]
    rows = cand_x.reshape(own_rows, D)
    place = jnp.stack([lax.axis_index("yh"), lax.axis_index("x"), lax.axis_index("c")]).astype(jnp.int32)
    y = lax.axis_index("yl").astype(jnp.int32)

    def along_y(values, step):
        return lax.ppermute(values, "yl", [(i, i ^ step) for i in range(4)])

    second = hist_kv[:, FIRST:]
    plane = exchange(hist_kv[:, :FIRST].reshape(8, 4, FIRST, 128), "z")
    other_rows, other_w = swap(rows, "yh"), swap(w_out, "yh")
    quads = go_round(jnp.stack([rows, other_rows]))
    other_w, *quads = lax.optimization_barrier((other_w, *quads))
    query, gate, message = project(place, hist_len, block_mask, quads, w_proj)
    messages = jnp.stack([message] + [along_y(message, step) for step in (1, 2, 3)])
    plane, second, query, gate, messages, other_w = lax.optimization_barrier(
        (plane, second, query, gate, messages, other_w)
    )
    rest = exchange(second, ("z", "yl"))

    live = messages[:, 256].astype(jnp.int32).reshape(4, 8, 4, 4)
    live = lax.dynamic_index_in_dim(live, y, 2, keepdims=False)[:, :, : -(-FIRST // BLK)]
    part = attend_plane(y.reshape(1), live.reshape(-1), messages, plane)
    sums = [part[0]] + [along_y(part[step], step) for step in (1, 2, 3)]
    w_quads = go_round(jnp.stack([w_out, other_w]))
    attended = attend_last(FIRST, 8, hist_len, block_mask, cand_count, query, rest, gate, sums)
    keep = cand_count - lax.axis_index(GRP) * own_rows
    parts = exchange(attended, GRP)
    return output(place, keep, parts, w_quads, rows).reshape(cand_x.shape)


def solution(mesh):
    split = Mesh(mesh.devices.reshape(2, 4, 2, 8, 4), ("yh", "x", "c", "z", "yl"))
    hist = ("z", "yl")
    in_specs = (
        P(GRP, hist, None),
        P(None, hist, GRP),
        P(hist),
        P(hist),
        P(hist, None),
        P(None, GRP),
        P(GRP, None),
    )
    return jax.shard_map(per_device, mesh=split, in_specs=in_specs, out_specs=P(GRP, hist, None), check_vma=False)
```

```python
import functools

import jax
import jax.numpy as jnp
from jax import lax
from jax.experimental import pallas as pl
from jax.experimental.pallas import tpu as pltpu
from jax.sharding import Mesh
from jax.sharding import PartitionSpec as P

D = 1024
BLK = 128
FINE = 64
FIRST = 384
GRP = ("yh", "x", "c")
HALF = 64
PARAMS = pltpu.CompilerParams(vmem_limit_bytes=24 * 1024 * 1024)


def layer_norm(values):
    average = jnp.mean(values, axis=-1, keepdims=True)
    centred = values - average
    spread = jnp.mean(centred * centred, axis=-1, keepdims=True)
    return centred * lax.rsqrt(spread + 1e-05)


def low_lanes(shape):
    return lax.broadcasted_iota(jnp.int32, shape, len(shape) - 1) < HALF


def member(place_ref, turns, core, half):
    yh, x, c = place_ref[0], place_ref[1], place_ref[2]
    return (yh ^ half) * 8 + lax.rem(x - turns + 4, 4) * 2 + (c ^ core)


def project_kernel(place_ref, length_ref, mask_ref, *refs):
    quads, (w_ref, query_ref, gate_ref, message_ref) = refs[:4], refs[4:]
    block = lax.broadcasted_iota(jnp.int32, (16, 128), 1)
    live = jnp.clip(length_ref[0] - block * BLK, 0, BLK) * mask_ref[...]
    message_ref[256:272] = live.astype(jnp.float32).astype(jnp.bfloat16)
    for turns, quad in enumerate(quads):
        _, _, own, width = quad.shape
        rows = quad[...].reshape(4 * own, width).astype(jnp.float32)
        normed = layer_norm(rows).astype(jnp.bfloat16)
        product = jnp.dot(normed, w_ref[...], preferred_element_type=jnp.float32)
        values = (product / (1.0 + jnp.exp(-product))).astype(jnp.bfloat16).astype(jnp.float32)
        query = jnp.where(low_lanes(values.shape), values * (0.5 * HALF ** (-0.5)), 0.0).astype(jnp.bfloat16)
        pairs = values.reshape(4, 2, own // 2, 128)
        first, second = pairs[:, 0], pairs[:, 1]
        turned = pltpu.roll(first.reshape(-1, 128), HALF, 1).reshape(first.shape)
        gate = jnp.where(low_lanes(first.shape), turned, second).astype(jnp.bfloat16)
        turned = pltpu.roll(second.reshape(-1, 128), HALF, 1).reshape(second.shape)
        packed = (jnp.where(low_lanes(first.shape), first, turned) * (0.5 * HALF ** (-0.5))).astype(jnp.bfloat16)
        for core in range(2):
            for half in range(2):
                at = member(place_ref, turns, core, half)
                block = core * 2 + half
                query_ref[pl.ds(pl.multiple_of(at * own, own), own)] = query[block * own : (block + 1) * own]
                gate_ref[at] = gate[block]
                message_ref[pl.ds(pl.multiple_of(at * 16, 16), 16)] = packed[block]


def project(place, length, mask, quads, w_proj):
    own = quads[0].shape[2]
    vmem = pl.BlockSpec(memory_space=pltpu.VMEM)
    return pl.pallas_call(
        project_kernel,
        out_shape=(
            jax.ShapeDtypeStruct((16 * own, 128), jnp.bfloat16),
            jax.ShapeDtypeStruct((16, own // 2, 128), jnp.bfloat16),
            jax.ShapeDtypeStruct((272, 128), jnp.bfloat16),
        ),
        in_specs=[pl.BlockSpec(memory_space=pltpu.SMEM)] * 2 + [vmem] * 6,
        out_specs=(vmem, vmem, vmem),
        compiler_params=PARAMS,
        cost_estimate=pl.CostEstimate(flops=2 * 512 * D * 128, bytes_accessed=2 << 20, transcendentals=0),
        name="project",
    )(place, length, mask, *quads, w_proj)


def attend_tiles(offset, y_ref, length_ref, mask_ref, count_ref, query_ref, kv_ref, total, masked):
    step = pl.program_id(0)
    sources, rows, _ = kv_ref.shape
    lives = []
    for source in range(sources):
        device = (step * (sources // 4) + source // 4) * 4 + (y_ref[0] ^ (source % 4))
        for block in range(rows // FINE):
            position = device * 512 + offset + block * FINE
            count = jnp.clip(length_ref[0] - position, 0, FINE)
            lives.append(count * mask_ref[0, device * 4 + (offset + block * FINE) // BLK])

    def attend_rows(chunks):
        row = lax.broadcasted_iota(jnp.int32, (FINE, 128), 0)
        for i, live in enumerate(lives):
            source, block = divmod(i, rows // FINE)
            piece = kv_ref[source, block * FINE : (block + 1) * FINE]
            masked[i * FINE : (i + 1) * FINE] = jnp.where(row < live, piece, jnp.zeros_like(piece))
        for start, end in chunks:
            scores = lax.dot_general(
                query_ref[start:end], masked[...], (((1,), (1,)), ((), ())), preferred_element_type=jnp.float32
            )
            weights = (scores + scores * jnp.tanh(scores)).astype(jnp.bfloat16)
            total[start:end] += jnp.dot(weights, masked[...], preferred_element_type=jnp.float32)

    some = functools.reduce(jnp.add, lives) > 0
    few = count_ref[0] <= 384

    @pl.when(jnp.logical_and(some, few))
    def _():
        attend_rows(((0, 256), (256, 384)))

    @pl.when(jnp.logical_and(some, jnp.logical_not(few)))
    def _():
        attend_rows(((0, 256), (256, 512)))


def attend_plane_kernel(y_ref, live_ref, message_ref, kv_ref, out_ref, masked):
    user = pl.program_id(0)
    planes, _, rows, _ = kv_ref.shape
    pieces = rows // FINE
    blocks = -(-rows // BLK)
    lives = []
    for plane in range(planes):
        for piece in range(pieces):
            block, part = divmod(piece * FINE, BLK)
            lives.append(jnp.clip(live_ref[(user * planes + plane) * blocks + block] - part, 0, FINE))
    some = functools.reduce(jnp.add, lives) > 0

    @pl.when(some)
    def _():
        row = lax.broadcasted_iota(jnp.int32, (FINE, 128), 0)
        for i, live in enumerate(lives):
            plane, piece = divmod(i, pieces)
            values = kv_ref[plane, 0, piece * FINE : (piece + 1) * FINE]
            masked[i * FINE : (i + 1) * FINE] = jnp.where(row < live, values, jnp.zeros_like(values))
        packed = message_ref[0, 0:256].astype(jnp.float32)
        low = low_lanes(packed.shape)
        totals = []
        for values in (packed, pltpu.roll(packed, HALF, 1)):
            query = jnp.where(low, values, 0.0).astype(jnp.bfloat16)
            scores = lax.dot_general(
                query, masked[...], (((1,), (1,)), ((), ())), preferred_element_type=jnp.float32
            )
            weights = (scores + scores * jnp.tanh(scores)).astype(jnp.bfloat16)
            totals.append(jnp.dot(weights, masked[...], preferred_element_type=jnp.float32))
        out_ref[0] = jnp.where(low, pltpu.roll(totals[0], HALF, 1), totals[1])

    @pl.when(jnp.logical_not(some))
    def _():
        out_ref[...] = jnp.zeros_like(out_ref)


def attend_plane(y, live, messages, kv):
    planes, users, rows, _ = kv.shape
    return pl.pallas_call(
        attend_plane_kernel,
        out_shape=jax.ShapeDtypeStruct((users, 256, 128), jnp.float32),
        grid_spec=pltpu.PrefetchScalarGridSpec(
            num_scalar_prefetch=1,
            grid=(users,),
            in_specs=[
                pl.BlockSpec(memory_space=pltpu.SMEM),
                pl.BlockSpec((1, 272, 128), lambda i, y: (i, 0, 0)),
                pl.BlockSpec((planes, 1, rows, 128), lambda i, y: (0, y[0] ^ i, 0, 0)),
            ],
            out_specs=pl.BlockSpec((1, 256, 128), lambda i, y: (i, 0, 0)),
            scratch_shapes=[pltpu.VMEM((planes * rows, 128), jnp.bfloat16)],
        ),
        compiler_params=PARAMS,
        cost_estimate=pl.CostEstimate(flops=1 << 30, bytes_accessed=3 << 20, transcendentals=1 << 22),
        name="attend_plane",
    )(y, live, messages, kv)


def attend_last_kernel(
    offset, y_ref, length_ref, mask_ref, count_ref, query_ref, kv_ref, gate_ref, a_ref, b_ref, c_ref, d_ref, out_ref, total, masked
):
    @pl.when(pl.program_id(0) == 0)
    def _():
        total[...] = jnp.zeros_like(total)

    attend_tiles(offset, y_ref, length_ref, mask_ref, count_ref, query_ref, kv_ref, total, masked)

    @pl.when(pl.program_id(0) == pl.num_programs(0) - 1)
    def _():
        slices = total[...].reshape(out_ref.shape[0], 2, 16, 128)
        first, second = slices[:, 0], slices[:, 1]
        turned = pltpu.roll(first.reshape(-1, 128), HALF, 1).reshape(first.shape)
        packed = jnp.where(low_lanes(first.shape), turned, second)
        others = a_ref[...] + b_ref[...] + c_ref[...] + d_ref[...]
        packed += others.reshape(packed.shape)
        high = packed.astype(jnp.bfloat16)
        out_ref[:, 0:16, :] = high
        out_ref[:, 16:32, :] = (packed - high.astype(jnp.float32)).astype(jnp.bfloat16)
        out_ref[:, 32:48, :] = gate_ref[...]


def attend_last(offset, sources, y, length, mask, cand_count, query, kv, gate, sums):
    count = query.shape[0]
    devices, rows, _ = kv.shape
    smem = pl.BlockSpec(memory_space=pltpu.SMEM)
    positions = devices * rows
    return pl.pallas_call(
        functools.partial(attend_last_kernel, offset),
        out_shape=jax.ShapeDtypeStruct((count // 32, 48, 128), jnp.bfloat16),
        grid=(devices // sources,),
        in_specs=[
            smem,
            smem,
            smem,
            smem,
            pl.BlockSpec((count, 128), lambda i: (0, 0)),
            pl.BlockSpec((sources, rows, 128), lambda i: (i, 0, 0)),
            pl.BlockSpec((count // 32, 16, 128), lambda i: (0, 0, 0)),
        ]
        + [pl.BlockSpec((256, 128), lambda i: (0, 0))] * 4,
        out_specs=pl.BlockSpec((count // 32, 48, 128), lambda i: (0, 0, 0)),
        scratch_shapes=[pltpu.VMEM((count, 128), jnp.float32), pltpu.VMEM((sources * rows, 128), jnp.bfloat16)],
        compiler_params=PARAMS,
        cost_estimate=pl.CostEstimate(
            flops=4 * count * positions * 128, bytes_accessed=positions * 256, transcendentals=count * positions
        ),
        name="attend_last",
    )(y, length, mask, cand_count, query, kv, gate, *sums)


def spread_heads(packed):
    columns = []
    for pair in range(len(packed) // 2):
        even, odd = packed[2 * pair], packed[2 * pair + 1]
        low = low_lanes(even.shape)
        top = jnp.where(low, even, pltpu.roll(odd, HALF, 1))
        bottom = jnp.where(low, pltpu.roll(even, HALF, 1), odd)
        columns.append(jnp.concatenate([top, bottom], axis=0))
    return jnp.concatenate(columns, axis=1)


def output_kernel(place_ref, count_ref, parts_ref, *refs):
    quads, (x_ref, out_ref) = refs[:4], refs[4:]
    attended, gate = [], []
    for turns in range(4):
        for core in range(2):
            for half in range(2):
                part = parts_ref[member(place_ref, turns, core, half)].astype(jnp.float32)
                attended.append(part[0:16] + part[16:32])
                gate.append(part[32:48])
    gated = (layer_norm(spread_heads(attended)) * spread_heads(gate)).astype(jnp.bfloat16)
    mixed = x_ref[...].astype(jnp.float32)
    for turns, quad in enumerate(quads):
        depth = 4 * quad.shape[2]
        weights = quad[...].reshape(depth, quad.shape[3])
        mixed += jnp.dot(gated[:, turns * depth : (turns + 1) * depth], weights, preferred_element_type=jnp.float32)
    row = lax.broadcasted_iota(jnp.int32, mixed.shape, 0)
    out_ref[...] = jnp.where(row < count_ref[0], mixed, 0.0).astype(jnp.bfloat16)


def output(place, keep, parts, quads, rows):
    smem, vmem = pl.BlockSpec(memory_space=pltpu.SMEM), pl.BlockSpec(memory_space=pltpu.VMEM)
    return pl.pallas_call(
        output_kernel,
        out_shape=jax.ShapeDtypeStruct(rows.shape, jnp.bfloat16),
        in_specs=[smem, smem] + [vmem] * 6,
        out_specs=vmem,
        compiler_params=PARAMS,
        cost_estimate=pl.CostEstimate(flops=2 * 32 * D * D, bytes_accessed=3 << 20, transcendentals=0),
        name="output",
    )(place, keep, parts, *quads, rows)


def exchange(values, axes):
    return lax.all_to_all(values, axes, split_axis=0, concat_axis=0, tiled=True)


def swap(values, axis):
    return lax.ppermute(values, axis, [(0, 1), (1, 0)])


def both_cores(own, other):
    pair = jnp.stack([own, other])
    return jnp.stack([pair, swap(pair, "c")])


def go_round(quad):
    return [quad] + [lax.ppermute(quad, "x", [(i, (i + turns) % 4) for i in range(4)]) for turns in (1, 2, 3)]


def per_device(cand_x, hist_kv, hist_len, cand_count, block_mask, w_proj, w_out):
    own_rows = cand_x.shape[0]
    rows = cand_x.reshape(own_rows, D)
    place = jnp.stack([lax.axis_index("yh"), lax.axis_index("x"), lax.axis_index("c")]).astype(jnp.int32)
    y = lax.axis_index("yl").astype(jnp.int32)

    def along_y(values, step):
        return lax.ppermute(values, "yl", [(i, i ^ step) for i in range(4)])

    second = hist_kv.reshape(8, 4, 512, 128)[:, :, FIRST:]
    plane = exchange(hist_kv[:, :FIRST].reshape(8, 4, FIRST, 128), "z")
    other_rows, other_w = swap(rows, "yh"), swap(w_out, "yh")
    quads = go_round(both_cores(rows, other_rows))
    second, _ = lax.optimization_barrier((second, other_rows))
    staged = [lax.dynamic_index_in_dim(second, y ^ step, 1, keepdims=False) for step in range(4)]
    staged = jnp.stack([staged[0]] + [along_y(staged[step], step) for step in (1, 2, 3)], axis=1)
    other_w, staged, *quads = lax.optimization_barrier((other_w, staged, *quads))
    query, gate, message = project(place, hist_len, block_mask, quads, w_proj)
    messages = jnp.stack([message] + [along_y(message, step) for step in (1, 2, 3)])
    live = messages[:, 256].astype(jnp.int32).reshape(4, 8, 4, 4)
    live = lax.dynamic_index_in_dim(live, y, 2, keepdims=False)[:, :, : -(-FIRST // BLK)].reshape(-1)
    message, other_w = lax.optimization_barrier((message, other_w))
    w_quad = both_cores(w_out, other_w)
    plane, staged, query, gate, messages, live, w_quad = lax.optimization_barrier(
        (plane, staged, query, gate, messages, live, w_quad)
    )
    rest = exchange(staged, "z").reshape(32, 512 - FIRST, 128)

    part = attend_plane(y.reshape(1), live, messages, plane)
    sums = [part[0]] + [along_y(part[step], step) for step in (1, 2, 3)]
    part, w_quad = lax.optimization_barrier((part, w_quad))
    w_quads = go_round(w_quad)
    attended = attend_last(FIRST, 16, y.reshape(1), hist_len, block_mask, cand_count, query, rest, gate, sums)
    keep = cand_count - lax.axis_index(GRP) * own_rows
    parts = exchange(attended, GRP)
    return output(place, keep, parts, w_quads, rows).reshape(cand_x.shape)


def solution(mesh):
    split = Mesh(mesh.devices.reshape(2, 4, 2, 8, 4), ("yh", "x", "c", "z", "yl"))
    hist = ("z", "yl")
    in_specs = (
        P(GRP, hist, None),
        P(None, hist, GRP),
        P(hist),
        P(hist),
        P(hist, None),
        P(None, GRP),
        P(GRP, None),
    )
    return jax.shard_map(per_device, mesh=split, in_specs=in_specs, out_specs=P(GRP, hist, None), check_vma=False)
```

```python
import functools

import jax
import jax.numpy as jnp
from jax import lax
from jax.experimental import pallas as pl
from jax.experimental.pallas import tpu as pltpu
from jax.sharding import Mesh
from jax.sharding import PartitionSpec as P

D = 1024
BLK = 128
FINE = 64
FIRST = 384
GRP = ("yh", "x", "c")
HALF = 64
PARAMS = pltpu.CompilerParams(vmem_limit_bytes=24 * 1024 * 1024)


def layer_norm(values):
    average = jnp.mean(values, axis=-1, keepdims=True)
    centred = values - average
    spread = jnp.mean(centred * centred, axis=-1, keepdims=True)
    return centred * lax.rsqrt(spread + 1e-05)


def low_lanes(shape):
    return lax.broadcasted_iota(jnp.int32, shape, len(shape) - 1) < HALF


def member(place_ref, turns, core, half):
    yh, x, c = place_ref[0], place_ref[1], place_ref[2]
    return (yh ^ half) * 8 + lax.rem(x - turns + 4, 4) * 2 + (c ^ core)


def project_kernel(place_ref, length_ref, mask_ref, *refs):
    quads, (w_ref, query_ref, gate_ref, message_ref) = refs[:4], refs[4:]
    block = lax.broadcasted_iota(jnp.int32, (16, 128), 1)
    live = jnp.clip(length_ref[0] - block * BLK, 0, BLK) * mask_ref[...]
    message_ref[256:272] = live.astype(jnp.float32).astype(jnp.bfloat16)
    for turns, quad in enumerate(quads):
        _, _, own, width = quad.shape
        rows = quad[...].reshape(4 * own, width).astype(jnp.float32)
        normed = layer_norm(rows).astype(jnp.bfloat16)
        product = jnp.dot(normed, w_ref[...], preferred_element_type=jnp.float32)
        values = (product / (1.0 + jnp.exp(-product))).astype(jnp.bfloat16).astype(jnp.float32)
        query = jnp.where(low_lanes(values.shape), values * (0.5 * HALF ** (-0.5)), 0.0).astype(jnp.bfloat16)
        pairs = values.reshape(4, 2, own // 2, 128)
        first, second = pairs[:, 0], pairs[:, 1]
        turned = pltpu.roll(first.reshape(-1, 128), HALF, 1).reshape(first.shape)
        gate = jnp.where(low_lanes(first.shape), turned, second).astype(jnp.bfloat16)
        turned = pltpu.roll(second.reshape(-1, 128), HALF, 1).reshape(second.shape)
        packed = (jnp.where(low_lanes(first.shape), first, turned) * (0.5 * HALF ** (-0.5))).astype(jnp.bfloat16)
        for core in range(2):
            for half in range(2):
                at = member(place_ref, turns, core, half)
                block = core * 2 + half
                query_ref[pl.ds(pl.multiple_of(at * own, own), own)] = query[block * own : (block + 1) * own]
                gate_ref[at] = gate[block]
                message_ref[pl.ds(pl.multiple_of(at * 16, 16), 16)] = packed[block]


def project(place, length, mask, quads, w_proj):
    own = quads[0].shape[2]
    vmem = pl.BlockSpec(memory_space=pltpu.VMEM)
    return pl.pallas_call(
        project_kernel,
        out_shape=(
            jax.ShapeDtypeStruct((16 * own, 128), jnp.bfloat16),
            jax.ShapeDtypeStruct((16, own // 2, 128), jnp.bfloat16),
            jax.ShapeDtypeStruct((272, 128), jnp.bfloat16),
        ),
        in_specs=[pl.BlockSpec(memory_space=pltpu.SMEM)] * 2 + [vmem] * 6,
        out_specs=(vmem, vmem, vmem),
        compiler_params=PARAMS,
        cost_estimate=pl.CostEstimate(flops=2 * 512 * D * 128, bytes_accessed=2 << 20, transcendentals=0),
        name="project",
    )(place, length, mask, *quads, w_proj)


def attend_tiles(offset, y_ref, length_ref, mask_ref, count_ref, query_ref, kv_ref, total, masked):
    step = pl.program_id(0)
    sources, rows, _ = kv_ref.shape
    lives = []
    for source in range(sources):
        device = (step * (sources // 4) + source // 4) * 4 + (y_ref[0] ^ (source % 4))
        for block in range(rows // FINE):
            position = device * 512 + offset + block * FINE
            count = jnp.clip(length_ref[0] - position, 0, FINE)
            lives.append(count * mask_ref[0, device * 4 + (offset + block * FINE) // BLK])

    def attend_rows(chunks):
        row = lax.broadcasted_iota(jnp.int32, (FINE, 128), 0)
        for i, live in enumerate(lives):
            source, block = divmod(i, rows // FINE)
            piece = kv_ref[source, block * FINE : (block + 1) * FINE]
            masked[i * FINE : (i + 1) * FINE] = jnp.where(row < live, piece, jnp.zeros_like(piece))
        for start, end in chunks:
            scores = lax.dot_general(
                query_ref[start:end], masked[...], (((1,), (1,)), ((), ())), preferred_element_type=jnp.float32
            )
            weights = (scores + scores * jnp.tanh(scores)).astype(jnp.bfloat16)
            total[start:end] += jnp.dot(weights, masked[...], preferred_element_type=jnp.float32)

    some = functools.reduce(jnp.add, lives) > 0
    few = count_ref[0] <= 384

    @pl.when(jnp.logical_and(some, few))
    def _():
        attend_rows(((0, 256), (256, 384)))

    @pl.when(jnp.logical_and(some, jnp.logical_not(few)))
    def _():
        attend_rows(((0, 256), (256, 512)))


def attend_plane_kernel(y_ref, live_ref, message_ref, kv_ref, out_ref, masked):
    user = pl.program_id(0)
    planes, _, rows, _ = kv_ref.shape
    pieces = rows // FINE
    blocks = -(-rows // BLK)
    lives = []
    for plane in range(planes):
        for piece in range(pieces):
            block, part = divmod(piece * FINE, BLK)
            lives.append(jnp.clip(live_ref[(user * planes + plane) * blocks + block] - part, 0, FINE))
    some = functools.reduce(jnp.add, lives) > 0

    @pl.when(some)
    def _():
        row = lax.broadcasted_iota(jnp.int32, (FINE, 128), 0)
        for i, live in enumerate(lives):
            plane, piece = divmod(i, pieces)
            values = kv_ref[plane, 0, piece * FINE : (piece + 1) * FINE]
            masked[i * FINE : (i + 1) * FINE] = jnp.where(row < live, values, jnp.zeros_like(values))
        packed = message_ref[0, 0:256].astype(jnp.float32)
        low = low_lanes(packed.shape)
        totals = []
        for values in (packed, pltpu.roll(packed, HALF, 1)):
            query = jnp.where(low, values, 0.0).astype(jnp.bfloat16)
            scores = lax.dot_general(
                query, masked[...], (((1,), (1,)), ((), ())), preferred_element_type=jnp.float32
            )
            weights = (scores + scores * jnp.tanh(scores)).astype(jnp.bfloat16)
            totals.append(jnp.dot(weights, masked[...], preferred_element_type=jnp.float32))
        out_ref[0] = jnp.where(low, pltpu.roll(totals[0], HALF, 1), totals[1])

    @pl.when(jnp.logical_not(some))
    def _():
        out_ref[...] = jnp.zeros_like(out_ref)


def attend_plane(y, live, messages, kv):
    planes, users, rows, _ = kv.shape
    return pl.pallas_call(
        attend_plane_kernel,
        out_shape=jax.ShapeDtypeStruct((users, 256, 128), jnp.float32),
        grid_spec=pltpu.PrefetchScalarGridSpec(
            num_scalar_prefetch=1,
            grid=(users,),
            in_specs=[
                pl.BlockSpec(memory_space=pltpu.SMEM),
                pl.BlockSpec((1, 272, 128), lambda i, y: (i, 0, 0)),
                pl.BlockSpec((planes, 1, rows, 128), lambda i, y: (0, y[0] ^ i, 0, 0)),
            ],
            out_specs=pl.BlockSpec((1, 256, 128), lambda i, y: (i, 0, 0)),
            scratch_shapes=[pltpu.VMEM((planes * rows, 128), jnp.bfloat16)],
        ),
        compiler_params=PARAMS,
        cost_estimate=pl.CostEstimate(flops=1 << 30, bytes_accessed=3 << 20, transcendentals=1 << 22),
        name="attend_plane",
    )(y, live, messages, kv)


def attend_last_kernel(
    offset, y_ref, length_ref, mask_ref, count_ref, query_ref, kv_ref, gate_ref, a_ref, b_ref, c_ref, d_ref, out_ref, total, masked
):
    @pl.when(pl.program_id(0) == 0)
    def _():
        total[...] = jnp.zeros_like(total)

    attend_tiles(offset, y_ref, length_ref, mask_ref, count_ref, query_ref, kv_ref, total, masked)

    @pl.when(pl.program_id(0) == pl.num_programs(0) - 1)
    def _():
        slices = total[...].reshape(out_ref.shape[0], 2, 16, 128)
        first, second = slices[:, 0], slices[:, 1]
        turned = pltpu.roll(first.reshape(-1, 128), HALF, 1).reshape(first.shape)
        packed = jnp.where(low_lanes(first.shape), turned, second)
        others = a_ref[...] + b_ref[...] + c_ref[...] + d_ref[...]
        packed += others.reshape(packed.shape)
        high = packed.astype(jnp.bfloat16)
        out_ref[:, 0:16, :] = high
        out_ref[:, 16:32, :] = (packed - high.astype(jnp.float32)).astype(jnp.bfloat16)
        out_ref[:, 32:48, :] = gate_ref[...]


def attend_last(offset, sources, y, length, mask, cand_count, query, kv, gate, sums):
    count = query.shape[0]
    devices, rows, _ = kv.shape
    smem = pl.BlockSpec(memory_space=pltpu.SMEM)
    positions = devices * rows
    return pl.pallas_call(
        functools.partial(attend_last_kernel, offset),
        out_shape=jax.ShapeDtypeStruct((count // 32, 48, 128), jnp.bfloat16),
        grid=(devices // sources,),
        in_specs=[
            smem,
            smem,
            smem,
            smem,
            pl.BlockSpec((count, 128), lambda i: (0, 0)),
            pl.BlockSpec((sources, rows, 128), lambda i: (i, 0, 0)),
            pl.BlockSpec((count // 32, 16, 128), lambda i: (0, 0, 0)),
        ]
        + [pl.BlockSpec((256, 128), lambda i: (0, 0))] * 4,
        out_specs=pl.BlockSpec((count // 32, 48, 128), lambda i: (0, 0, 0)),
        scratch_shapes=[pltpu.VMEM((count, 128), jnp.float32), pltpu.VMEM((sources * rows, 128), jnp.bfloat16)],
        compiler_params=PARAMS,
        cost_estimate=pl.CostEstimate(
            flops=4 * count * positions * 128, bytes_accessed=positions * 256, transcendentals=count * positions
        ),
        name="attend_last",
    )(y, length, mask, cand_count, query, kv, gate, *sums)


def spread_heads(packed):
    columns = []
    for pair in range(len(packed) // 2):
        even, odd = packed[2 * pair], packed[2 * pair + 1]
        low = low_lanes(even.shape)
        top = jnp.where(low, even, pltpu.roll(odd, HALF, 1))
        bottom = jnp.where(low, pltpu.roll(even, HALF, 1), odd)
        columns.append(jnp.concatenate([top, bottom], axis=0))
    return jnp.concatenate(columns, axis=1)


def output_kernel(place_ref, count_ref, parts_ref, *refs):
    quads, (x_ref, out_ref) = refs[:4], refs[4:]
    attended, gate = [], []
    for turns in range(4):
        for core in range(2):
            for half in range(2):
                part = parts_ref[member(place_ref, turns, core, half)].astype(jnp.float32)
                attended.append(part[0:16] + part[16:32])
                gate.append(part[32:48])
    gated = (layer_norm(spread_heads(attended)) * spread_heads(gate)).astype(jnp.bfloat16)
    mixed = x_ref[...].astype(jnp.float32)
    for turns, quad in enumerate(quads):
        depth = 4 * quad.shape[2]
        weights = quad[...].reshape(depth, quad.shape[3])
        mixed += jnp.dot(gated[:, turns * depth : (turns + 1) * depth], weights, preferred_element_type=jnp.float32)
    row = lax.broadcasted_iota(jnp.int32, mixed.shape, 0)
    out_ref[...] = jnp.where(row < count_ref[0], mixed, 0.0).astype(jnp.bfloat16)


def output(place, keep, parts, quads, rows):
    smem, vmem = pl.BlockSpec(memory_space=pltpu.SMEM), pl.BlockSpec(memory_space=pltpu.VMEM)
    return pl.pallas_call(
        output_kernel,
        out_shape=jax.ShapeDtypeStruct(rows.shape, jnp.bfloat16),
        in_specs=[smem, smem] + [vmem] * 6,
        out_specs=vmem,
        compiler_params=PARAMS,
        cost_estimate=pl.CostEstimate(flops=2 * 32 * D * D, bytes_accessed=3 << 20, transcendentals=0),
        name="output",
    )(place, keep, parts, *quads, rows)


def exchange(values, axes):
    return lax.all_to_all(values, axes, split_axis=0, concat_axis=0, tiled=True)


def swap(values, axis):
    return lax.ppermute(values, axis, [(0, 1), (1, 0)])


def both_cores(own, other):
    pair = jnp.stack([own, other])
    return jnp.stack([pair, swap(pair, "c")])


def go_round(quad):
    return [quad] + [lax.ppermute(quad, "x", [(i, (i + turns) % 4) for i in range(4)]) for turns in (1, 2, 3)]


def per_device(cand_x, hist_kv, hist_len, cand_count, block_mask, w_proj, w_out):
    own_rows = cand_x.shape[0]
    rows = cand_x.reshape(own_rows, D)
    place = jnp.stack([lax.axis_index("yh"), lax.axis_index("x"), lax.axis_index("c")]).astype(jnp.int32)
    y = lax.axis_index("yl").astype(jnp.int32)

    def along_y(values, step):
        return lax.ppermute(values, "yl", [(i, i ^ step) for i in range(4)])

    second = hist_kv.reshape(8, 4, 512, 128)[:, :, FIRST:]
    plane = exchange(hist_kv[:, :FIRST].reshape(8, 4, FIRST, 128), "z")
    other = swap(jnp.concatenate([rows, w_out]), "yh")
    other_rows, other_w = other[:own_rows], other[own_rows:]
    quads = go_round(both_cores(rows, other_rows))
    second, _ = lax.optimization_barrier((second, other))
    staged = [lax.dynamic_index_in_dim(second, y ^ step, 1, keepdims=False) for step in range(4)]
    staged = jnp.stack([staged[0]] + [along_y(staged[step], step) for step in (1, 2, 3)], axis=1)
    other_w, staged, *quads = lax.optimization_barrier((other_w, staged, *quads))
    query, gate, message = project(place, hist_len, block_mask, quads, w_proj)
    messages = jnp.stack([message] + [along_y(message, step) for step in (1, 2, 3)])
    live = messages[:, 256].astype(jnp.int32).reshape(4, 8, 4, 4)
    live = lax.dynamic_index_in_dim(live, y, 2, keepdims=False)[:, :, : -(-FIRST // BLK)].reshape(-1)
    message, other_w = lax.optimization_barrier((message, other_w))
    w_quad = both_cores(w_out, other_w)
    plane, staged, query, gate, messages, live, w_quad = lax.optimization_barrier(
        (plane, staged, query, gate, messages, live, w_quad)
    )
    rest = exchange(staged, "z").reshape(32, 512 - FIRST, 128)

    part = attend_plane(y.reshape(1), live, messages, plane)
    sums = [part[0]] + [along_y(part[step], step) for step in (1, 2, 3)]
    part, w_quad = lax.optimization_barrier((part, w_quad))
    w_quads = go_round(w_quad)
    attended = attend_last(FIRST, 16, y.reshape(1), hist_len, block_mask, cand_count, query, rest, gate, sums)
    keep = cand_count - lax.axis_index(GRP) * own_rows
    parts = exchange(attended, GRP)
    return output(place, keep, parts, w_quads, rows).reshape(cand_x.shape)


def solution(mesh):
    split = Mesh(mesh.devices.reshape(2, 4, 2, 8, 4), ("yh", "x", "c", "z", "yl"))
    hist = ("z", "yl")
    in_specs = (
        P(GRP, hist, None),
        P(None, hist, GRP),
        P(hist),
        P(hist),
        P(hist, None),
        P(None, GRP),
        P(GRP, None),
    )
    return jax.shard_map(per_device, mesh=split, in_specs=in_specs, out_specs=P(GRP, hist, None), check_vma=False)
```
